32 devices in a mesh: grp: 2 (over y), edge: 4 (over z), feat: 2 (over x), rep: 2 (over core).
Axes of the slice: x: 2, y: 2, z: 4, core: 2. Of those that a mesh axis runs over, the one named last changes fastest.
Arguments:
- edge_embed: bfloat16 [8192, 512], P(('grp', 'edge'), 'feat'), parts along dimension 0, may hold values from -6 to 6
- w_down: bfloat16 [512, 64], P('feat'), may hold values from -0.25 to 0.25
- w_bilinear: bfloat16 [64, 64], replicated, may hold values from -0.75 to 0.75
- w_up: bfloat16 [64, 512], P(None, 'feat'), may hold values from -0.75 to 0.75
- w_residual: bfloat16 [2, 512, 512], replicated, may hold values from -0.25 to 0.25
- tile_coef: bfloat16 [64, 16, 128, 128], P(('grp', 'edge'), 'rep'), parts along dimension 0, may hold values from -0.125 to 0.125
- tile_source: int32 [64, 16], P('grp'), parts along dimension 0, may hold values from 0 to 31, as said below
- target_rows: int32 [8192], P(('grp', 'edge')), parts along dimension 0, may hold values from 0 to 4095, as said below
- cotangent: bfloat16 [8192, 512], P(('grp', 'edge'), 'feat'), parts along dimension 0, may hold values from -6 to 6
Outputs:
- edge_out: bfloat16 [8192, 512], P(('grp', 'edge'), 'feat'), parts along dimension 0
- grad_target: bfloat16 [8192, 512], P(('grp', 'edge'), 'feat'), parts along dimension 0
The draws below stay inside these ranges and needn't reach their ends.
There are 2 independent parts, one for each index of `grp`. The reference program is written for one: setup_inputs(seed, part) draws one part's arguments, and reference() takes and returns one part's arrays. A program takes and returns all parts, laid end to end along the dimension named above; an argument that names none is the same for every part. Nothing has to cross between parts.
Inputs may be any that keep to these rules, and one draw needn't show every extreme that they name: `tile_source`: blocks t*8 to t*8 + 7 belong to index t of the edge axis; tiles r*8 to r*8 + 7 belong to index r of rep. Among the 64 tiles of one edge index and one rep index, at most 32 name blocks of any one edge index, and exactly 32 name blocks of some edge index. `target_rows`: row t = q*1024 + p*256 + l with l < 256 names a source row p*1024 + q*256 + l2 with l2 < 256; every source row is named once.
All inputs are finite; a program needn't handle non-finite values.
Results may differ from the reference program's by a relative error of at most 0.0085.
Values may be sent and summed in bfloat16 or wider, within the bound.
A program may use at most 64 MiB of HBM per device.

```python
import jax
import jax.numpy as jnp
from jax import lax

D = 512
DT = 64
B = 128
BLK_DEV = 8
KH = 8
L = 2
K = 16
E_DEV = 1024
NB = 32
E = 4096
CAP = 32
SPAN = 256
N_EDGE = 4
N_REP = 2


def draw_tile_source(key, part):
    key = jax.random.fold_in(key, 11)
    groups = N_EDGE * N_REP
    entries = BLK_DEV * KH
    half = CAP // 2
    key_perm, key_move, key_order, key_local = jax.random.split(key, 4)
    owner_perm = jax.vmap(lambda sub: jax.random.permutation(sub, N_EDGE))(jax.random.split(key_perm, groups))
    moves = jax.random.randint(key_move, (groups, N_EDGE // 2), -half, half + 1)
    moves = moves.at[:, 0].set(half)
    counts = jnp.stack([half + moves, half - moves], axis=2).reshape(groups, N_EDGE)
    bounds = jnp.cumsum(counts, axis=1)
    positions = jnp.arange(entries, dtype=jnp.int32)
    slot_pos = jnp.sum((bounds[:, None, :] <= positions[None, :, None]).astype(jnp.int32), axis=2)
    owners = jnp.take_along_axis(owner_perm, slot_pos, axis=1)
    shuffle = jax.vmap(lambda sub: jax.random.permutation(sub, entries))(jax.random.split(key_order, groups))
    owners = jnp.take_along_axis(owners, shuffle, axis=1)
    local_ids = jax.random.randint(key_local, (groups, entries), 0, BLK_DEV)
    ids = (owners * BLK_DEV + local_ids).astype(jnp.int32)
    ids = ids.reshape(N_EDGE, N_REP, BLK_DEV, KH).transpose(0, 2, 1, 3)
    return ids.reshape(NB, K)


def draw_target_rows(key, part):
    key = jax.random.fold_in(key, 23)
    perms = jax.vmap(lambda sub: jax.random.permutation(sub, SPAN))(jax.random.split(key, N_EDGE * N_EDGE))
    perms = perms.reshape(N_EDGE, N_EDGE, SPAN)
    dest = jnp.arange(N_EDGE, dtype=jnp.int32)[:, None, None]
    anchor = jnp.arange(N_EDGE, dtype=jnp.int32)[None, :, None]
    rows = anchor * E_DEV + dest * SPAN + perms
    return rows.reshape(E).astype(jnp.int32)


def levels(own_key, shape, pieces, least, largest):
    loudness, own = 1.0, jax.random.fold_in(own_key, 6)
    for axis_at, parts in pieces:
        draws = jnp.exp(jax.random.uniform(jax.random.fold_in(own, axis_at), (parts,), jnp.float32, least / len(pieces), largest / len(pieces)))
        loudness = loudness * jnp.repeat(draws, shape[axis_at] // parts).reshape([-1 if axis == axis_at else 1 for axis in range(len(shape))])
    return loudness


def bell_draw(key, shape, deviation, most, cuts=(), kind=jnp.bfloat16):
    drawn = deviation * jax.random.normal(key, shape, jnp.float32)
    if cuts:
        drawn = drawn * levels(key, shape, cuts, -0.22, 0.18)
    return jnp.clip(drawn, -most, most).astype(kind)


def setup_inputs(seed: int = 0, part: int = 0) -> dict:
    splits = jax.random.split(jax.random.key(seed), 10)
    part_keys = jax.random.split(jax.random.fold_in(splits[9], part), 10)
    return {
        "edge_embed": bell_draw(part_keys[0], (E, D), 1.0, 6.0, ((0, 4), (1, 2))),
        "w_down": bell_draw(splits[1], (D, DT), D ** -0.5, 0.25, ((0, 2),)),
        "w_bilinear": bell_draw(splits[2], (DT, DT), DT ** -0.5, 0.75),
        "w_up": bell_draw(splits[3], (DT, D), DT ** -0.5, 0.75, ((1, 2),)),
        "w_residual": bell_draw(splits[4], (L, D, D), D ** -0.5, 0.25),
        "tile_coef": bell_draw(part_keys[5], (NB, K, B, B), (B * K) ** -0.5, 0.125, ((0, 4), (1, 2))),
        "tile_source": draw_tile_source(jax.random.fold_in(jax.random.fold_in(splits[9], part), 71), part),
        "target_rows": draw_target_rows(jax.random.fold_in(jax.random.fold_in(splits[9], part), 71), part),
        "cotangent": bell_draw(part_keys[8], (E, D), 1.0, 6.0, ((0, 4), (1, 2))),
    }


def silu_slope(value):
    sig = jax.nn.sigmoid(value)
    return sig * (1.0 + value * (1.0 - sig))


def reference(edge_embed, w_down, w_bilinear, w_up, w_residual, tile_coef, tile_source, target_rows, cotangent):
    pre_down = jnp.dot(edge_embed, w_down, preferred_element_type=jnp.float32)
    down = jax.nn.silu(pre_down).astype(jnp.bfloat16)
    block_table = down.reshape(NB, B, DT)

    def forward_block(item):
        coef_block, source_ids = item
        sources = block_table[source_ids]
        return jnp.einsum("kij,kjc->ic", coef_block.astype(jnp.float32), sources.astype(jnp.float32))

    tri_sum = lax.map(forward_block, (tile_coef, tile_source)).reshape(E, DT).astype(jnp.bfloat16)
    pre_bil = jnp.dot(tri_sum, w_bilinear, preferred_element_type=jnp.float32)
    mid_act = jax.nn.silu(pre_bil).astype(jnp.bfloat16)
    hidden = (edge_embed.astype(jnp.float32) + jnp.dot(mid_act, w_up, preferred_element_type=jnp.float32)).astype(jnp.bfloat16)
    saved = []
    for layer in range(L):
        pre_res = jnp.dot(hidden, w_residual[layer], preferred_element_type=jnp.float32)
        hidden = (hidden.astype(jnp.float32) + jax.nn.silu(pre_res)).astype(jnp.bfloat16)
        saved.append(pre_res)
    edge_out = hidden

    grad_hidden = cotangent.astype(jnp.float32)
    for layer in range(L - 1, -1, -1):
        dz_layer = (grad_hidden * silu_slope(saved[layer])).astype(jnp.bfloat16)
        grad_hidden = grad_hidden + jnp.dot(dz_layer, w_residual[layer].T, preferred_element_type=jnp.float32)
    grad_hb = grad_hidden.astype(jnp.bfloat16)
    grad_mid = jnp.dot(grad_hb, w_up.T, preferred_element_type=jnp.float32)
    grad_bil = (grad_mid * silu_slope(pre_bil)).astype(jnp.bfloat16)
    grad_tri = jnp.dot(grad_bil, w_bilinear.T, preferred_element_type=jnp.float32).astype(jnp.bfloat16)
    grad_blocks = grad_tri.reshape(NB, B, DT)

    def backward_block(item):
        coef_block, grad_block = item
        return jnp.einsum("kij,ic->kjc", coef_block.astype(jnp.float32), grad_block.astype(jnp.float32)).astype(jnp.bfloat16)

    contrib = lax.map(backward_block, (tile_coef, grad_blocks))
    grad_down = jnp.zeros((NB, B, DT), jnp.float32).at[tile_source.reshape(-1)].add(contrib.reshape(NB * K, B, DT).astype(jnp.float32))
    grad_pre = (grad_down.reshape(E, DT) * silu_slope(pre_down)).astype(jnp.bfloat16)
    grad_edge = (grad_hb.astype(jnp.float32) + jnp.dot(grad_pre, w_down.T, preferred_element_type=jnp.float32)).astype(jnp.bfloat16)
    grad_target = grad_edge[target_rows]
    return edge_out, grad_target
```

```python
import functools

import jax
import jax.numpy as jnp
from jax import lax
from jax.experimental import pallas as pl
from jax.experimental.pallas import tpu as pltpu
from jax.sharding import PartitionSpec as P

MESH = pl.DeviceIdType.MESH
F32 = jnp.float32
BF16 = jnp.bfloat16


def mm(a, b, ca, cb):
    return lax.dot_general(a, b, (((ca,), (cb,)), ((), ())), preferred_element_type=F32)


def slope(value):
    sig = jax.nn.sigmoid(value)
    return sig * (1.0 + value * (1.0 - sig))


def block_kernel(
    n_edge,
    source,
    links,
    wanted,
    w_bil,
    edge_hbm,
    down_hbm,
    up_hbm,
    res_hbm,
    coef_hbm,
    cot_hbm,
    edge_out,
    grad_out,
    emb,
    cot,
    w_down,
    w_up,
    w_res,
    coef,
    down_mine,
    table,
    tri_part,
    tri_in,
    bil_mine,
    grad_tri,
    chain,
    pair_out,
    pair_in,
    red_out,
    red_in,
    out_mine,
    ge,
    turned,
    grad_v,
    local_sem,
    x_send,
    x_recv,
    tab_send,
    tab_recv,
    core_send,
    core_recv,
    tri_send,
    tri_recv,
    bil_send,
    bil_recv,
    pair_send,
    pair_recv,
    red_send,
    red_recv,
    out_send,
    out_recv,
    ge_send,
    ge_recv,
    fin_send,
    fin_recv,
    fin_local,
):
    g = lax.axis_index("grp")
    e = lax.axis_index("edge")
    f = lax.axis_index("feat")
    r = lax.axis_index("rep")
    of = 1 - f
    orr = 1 - r
    s = 2 * f + r
    blocks, tiles, rows_b, _ = coef.shape
    bpd = blocks // 4
    rows = emb.shape[1]
    half_c = table.shape[1]
    span = turned.shape[0] // n_edge
    spd = rows // span
    hs = span // 2

    def peer(d, df, dr):
        return (g, lax.rem(e + d, n_edge), of if df else f, orr if dr else r)

    def remote(src, dst, ss, rs, dev):
        return pltpu.make_async_remote_copy(
            src_ref=src, dst_ref=dst, send_sem=ss, recv_sem=rs, device_id=dev, device_id_type=MESH
        )

    def mine(who):
        return pl.ds(who * rows, rows)

    local = [
        pltpu.make_async_copy(down_hbm, w_down.at[f], local_sem.at[0]),
        pltpu.make_async_copy(edge_hbm.at[mine(s)], emb.at[f], local_sem.at[1]),
        pltpu.make_async_copy(up_hbm, w_up.at[f], local_sem.at[2]),
        pltpu.make_async_copy(coef_hbm, coef, local_sem.at[3]),
        pltpu.make_async_copy(res_hbm, w_res, local_sem.at[4]),
        pltpu.make_async_copy(cot_hbm.at[mine(s)], cot.at[f], local_sem.at[5]),
    ]
    for copy in local:
        copy.start()

    barrier = pltpu.get_barrier_semaphore()
    others = 0
    for d in range(n_edge):
        for df in range(2):
            for dr in range(2):
                if d or df or dr:
                    pl.semaphore_signal(
                        barrier, inc=1, device_id=peer(d, df, dr), device_id_type=MESH
                    )
                    others += 1
    pl.semaphore_wait(barrier, others)

    across = peer(0, 1, 0)
    partner_rows = mine(2 * of + r)
    xs = [
        remote(down_hbm, w_down.at[f], x_send.at[0], x_recv.at[0], across),
        remote(edge_hbm.at[partner_rows], emb.at[f], x_send.at[1], x_recv.at[1], across),
        remote(up_hbm, w_up.at[f], x_send.at[2], x_recv.at[2], across),
        remote(cot_hbm.at[partner_rows], cot.at[f], x_send.at[3], x_recv.at[3], across),
    ]
    for copy in xs:
        copy.start()
    local[0].wait()
    local[1].wait()
    xs[0].wait_recv()
    xs[1].wait_recv()
    embed = jnp.concatenate([emb[0], emb[1]], axis=1)
    wd = jnp.concatenate([w_down[0], w_down[1]], axis=0)
    pre_down = mm(wd, embed, 0, 1)
    down = jax.nn.silu(pre_down).astype(BF16)
    for h in range(2):
        for b in range(bpd):
            down_mine[h, b] = down[h * half_c : (h + 1) * half_c, b * rows_b : (b + 1) * rows_b]

    def region(ed, who):
        return pl.ds(ed * blocks + who * bpd, bpd)

    tabs = []
    for i in range(1, 2 * n_edge):
        d, df = i // 2, i % 2
        copy = remote(
            down_mine.at[of if df else f],
            table.at[region(e, s)],
            tab_send.at[i],
            tab_recv.at[i],
            peer(d, df, 0),
        )
        copy.start()
        tabs.append(copy)
    own = remote(
        down_mine.at[f], table.at[region(e, s)], core_send.at[0], core_recv.at[0], peer(0, 0, 1)
    )
    own.start()
    table[region(e, s)] = down_mine[f]
    cores = [own]
    for i in range(1, 2 * n_edge):
        d, df = i // 2, i % 2
        tabs[i - 1].wait_recv()
        place = region(lax.rem(e + n_edge - d, n_edge), 2 * (of if df else f) + r)
        copy = remote(
            table.at[place], table.at[place], core_send.at[i], core_recv.at[i], peer(0, 0, 1)
        )
        copy.start()
        cores.append(copy)
    local[3].wait()
    for copy in cores:
        copy.wait_recv()

    def forward(n, _):
        total = jnp.zeros((half_c, rows_b), F32)
        for k in range(tiles):
            total += mm(table[source[e * blocks + n, r * tiles + k]], coef[n, k], 1, 1)
        tri_part[n] = total
        return 0

    lax.fori_loop(0, blocks, forward, 0)
    tris = []
    for i in range(1, 4):
        df, dr = i // 2, i % 2
        to = 2 * (of if df else f) + (orr if dr else r)
        copy = remote(
            tri_part.at[pl.ds(to * bpd, bpd)],
            tri_in.at[i],
            tri_send.at[i],
            tri_recv.at[i],
            peer(0, df, dr),
        )
        copy.start()
        tris.append(copy)
    for copy in tris:
        copy.wait_recv()
    near = tri_part[pl.ds(s * bpd, bpd)] + tri_in[1]
    far = tri_in[2] + tri_in[3]
    low = jnp.where(f == 0, near, far)
    high = jnp.where(f == 0, far, near)
    tri = jnp.concatenate(
        [jnp.concatenate([low[b], high[b]], axis=0) for b in range(bpd)], axis=1
    ).astype(BF16)
    wb = w_bil[...]
    pre_bil = mm(wb, tri, 0, 0)
    mid = jax.nn.silu(pre_bil).astype(BF16)
    local[2].wait()
    xs[2].wait_recv()
    wu = jnp.concatenate([w_up[0], w_up[1]], axis=1)
    hidden = (embed.astype(F32) + mm(mid, wu, 0, 0)).astype(BF16)
    local[4].wait()
    saved = []
    for layer in range(w_res.shape[0]):
        pre = mm(hidden, w_res[layer], 1, 0)
        hidden = (hidden.astype(F32) + jax.nn.silu(pre)).astype(BF16)
        saved.append(slope(pre))
    cols = emb.shape[2]
    for h in range(2):
        out_mine[h] = hidden[:, h * cols : (h + 1) * cols]
    outs = []
    for i in range(1, 4):
        df, dr = i // 2, i % 2
        copy = remote(
            out_mine.at[of if df else f],
            edge_out.at[mine(s)],
            out_send.at[i],
            out_recv.at[i],
            peer(0, df, dr),
        )
        outs.append(copy)
    out_local = pltpu.make_async_copy(out_mine.at[f], edge_out.at[mine(s)], local_sem.at[6])
    out_local.start()
    local[5].wait()
    xs[3].wait_recv()
    grad = jnp.concatenate([cot[0], cot[1]], axis=1).astype(F32)
    for layer in range(w_res.shape[0] - 1, -1, -1):
        dz = (grad * saved[layer]).astype(BF16)
        grad = grad + mm(dz, w_res[layer], 1, 1)
    grad_hb = grad.astype(BF16)
    grad_bil = (mm(wu, grad_hb, 1, 1) * slope(pre_bil)).astype(BF16)
    grad_t = mm(wb, grad_bil, 1, 0).astype(BF16)
    for h in range(2):
        for b in range(bpd):
            bil_mine[h, b] = grad_t[h * half_c : (h + 1) * half_c, b * rows_b : (b + 1) * rows_b]
    bils = []
    for i in range(1, 4):
        df, dr = i // 2, i % 2
        copy = remote(
            bil_mine.at[of if df else f],
            grad_tri.at[pl.ds(s * bpd, bpd)],
            bil_send.at[i],
            bil_recv.at[i],
            peer(0, df, dr),
        )
        copy.start()
        bils.append(copy)
    for copy in outs:
        copy.start()
    grad_tri[pl.ds(s * bpd, bpd)] = bil_mine[f]
    chain[0] = jnp.zeros((half_c, rows_b), F32)
    for copy in bils:
        copy.wait_recv()

    def backward(n, _):
        block = grad_tri[n]
        parts = [mm(block, coef[n, k], 1, 0) for k in range(tiles)]
        for k in range(tiles):
            t = n * tiles + k
            chain[t + 1] = parts[k] + chain[links[t]]
        return 0

    lax.fori_loop(0, blocks, backward, 0)
    entries = blocks * tiles
    for i in range(2 * n_edge):
        for b in range(bpd):
            block_id = (i // 2) * blocks + (2 * (i % 2) + orr) * bpd + b
            pair_out[i, b] = chain[links[entries + block_id]]
    pair = remote(pair_out, pair_in, pair_send, pair_recv, peer(0, 0, 1))
    pair.start()
    pair.wait_recv()
    for i in range(2 * n_edge):
        for b in range(bpd):
            block_id = (i // 2) * blocks + (2 * (i % 2) + r) * bpd + b
            red_out[i, b] = (chain[links[entries + block_id]] + pair_in[i, b]).astype(BF16)
    reds = []
    for i in range(1, 2 * n_edge):
        d, df = i // 2, i % 2
        slot = 2 * lax.rem(e + d, n_edge) + (of if df else f)
        copy = remote(
            red_out.at[slot], red_in.at[i], red_send.at[i], red_recv.at[i], peer(d, df, 0)
        )
        copy.start()
        reds.append(copy)
    for copy in reds:
        copy.wait_recv()
    near = red_out[2 * e + f].astype(F32)
    far = red_in[1].astype(F32)
    for d in range(1, n_edge):
        near += red_in[2 * d].astype(F32)
        far += red_in[2 * d + 1].astype(F32)
    low = jnp.where(f == 0, near, far)
    high = jnp.where(f == 0, far, near)
    grad_down = jnp.concatenate(
        [jnp.concatenate([low[b], high[b]], axis=0) for b in range(bpd)], axis=1
    )
    grad_pre = (grad_down * slope(pre_down)).astype(BF16)
    grad_edge = (grad_hb.astype(F32) + mm(grad_pre, wd, 0, 1)).astype(BF16)
    for h in range(2):
        ge[h] = grad_edge[:, h * cols : (h + 1) * cols]

    sends = []
    for j in range(spd):
        q = s * spd + j
        d = lax.rem(q - e + n_edge, n_edge)
        for df in range(2):
            for dr in range(2):
                rt = orr if dr else r
                fr = of if df else f
                src = ge.at[fr, pl.ds(j * span + rt * hs, hs)]
                dst = turned.at[pl.ds(e * span + rt * hs, hs)]
                copy = remote(
                    src,
                    dst,
                    ge_send.at[j, 2 * df + dr],
                    ge_recv.at[d],
                    (g, q, fr, rt),
                )
                if df or dr:
                    copy.start()
                    sends.append((copy, None))
                else:
                    keep = pltpu.make_async_copy(src, dst, fin_local)

                    @pl.when(q == e)
                    def _(keep=keep):
                        keep.start()
                        keep.wait()

                    @pl.when(q != e)
                    def _(copy=copy):
                        copy.start()

                    sends.append((copy, q != e))
    fins = []
    for d in range(n_edge):
        p = lax.rem(e + n_edge - d, n_edge)
        place = pl.ds(p * span + r * hs, hs)
        arrive = remote(
            turned.at[place], turned.at[place], ge_send.at[0, 0], ge_recv.at[d], peer(0, 0, 1)
        )
        if d:
            arrive.wait_recv()
        else:

            @pl.when(s != e // spd)
            def _(arrive=arrive):
                arrive.wait_recv()

        copy = remote(
            turned.at[place], turned.at[place], fin_send.at[d], fin_recv.at[d], peer(0, 0, 1)
        )
        copy.start()
        fins.append(copy)
    writes = []
    for d in range(n_edge):
        p = lax.rem(e + n_edge - d, n_edge)
        fins[d].wait_recv()
        wish = wanted[p]
        slot = lax.broadcasted_iota(jnp.int32, (span, span), 0)
        pick = jnp.where(slot == wish, 1.0, 0.0).astype(BF16)
        place = pl.ds(p * span, span)
        grad_v[place] = mm(pick, turned[place], 0, 0).astype(BF16)
        copy = pltpu.make_async_copy(grad_v.at[place], grad_out.at[place], local_sem.at[7 + d])
        copy.start()
        writes.append(copy)
    for copy in outs:
        copy.wait()
    out_local.wait()
    for copy in xs + tabs + cores + tris + bils + [pair] + reds + fins:
        copy.wait_send()
    for copy, when in sends:
        if when is None:
            copy.wait_send()
        else:

            @pl.when(when)
            def _(copy=copy):
                copy.wait_send()

    for copy in writes:
        copy.wait()


def fused(
    edge_embed, w_down, w_bilinear, w_up, w_residual, tile_coef, tile_source, target_rows, cotangent
):
    n_edge = lax.axis_size("edge")
    edges, cols = edge_embed.shape
    blocks, tiles, rows_b, _ = tile_coef.shape
    width = w_down.shape[1]
    half_c = width // 2
    bpd = blocks // 4
    rows = edges // 4
    span = edges // n_edge
    n_blocks = n_edge * blocks
    entries = blocks * tiles
    mine = lax.dynamic_slice(
        tile_source,
        (lax.axis_index("edge") * blocks, lax.axis_index("rep") * tiles),
        (blocks, tiles),
    ).reshape(entries)
    asked = jnp.concatenate([mine, jnp.arange(n_blocks, dtype=jnp.int32)])
    before = jnp.concatenate(
        [jnp.arange(entries, dtype=jnp.int32), jnp.full((n_blocks,), entries, jnp.int32)]
    )
    order = jnp.arange(entries, dtype=jnp.int32)
    same = (asked[:, None] == mine[None, :]) & (order[None, :] < before[:, None])
    links = jnp.max(jnp.where(same, order[None, :] + 1, 0), axis=1)
    wanted = (target_rows % span).reshape(n_edge, 1, span)
    vmem = pl.BlockSpec(memory_space=pltpu.VMEM)
    smem = pl.BlockSpec(memory_space=pltpu.SMEM)
    hbm = pl.BlockSpec(memory_space=pl.ANY)
    dma = pltpu.SemaphoreType.DMA
    tile = (bpd, half_c, rows_b)
    n2 = 2 * n_edge
    return pl.pallas_call(
        functools.partial(block_kernel, n_edge),
        out_shape=[jax.ShapeDtypeStruct((edges, cols), BF16)] * 2,
        in_specs=[smem, smem, vmem, vmem] + [hbm] * 6,
        out_specs=[hbm, hbm],
        scratch_shapes=[
            pltpu.VMEM((2, rows, cols), BF16),
            pltpu.VMEM((2, rows, cols), BF16),
            pltpu.VMEM((2,) + w_down.shape, BF16),
            pltpu.VMEM((2,) + w_up.shape, BF16),
            pltpu.VMEM(w_residual.shape, BF16),
            pltpu.VMEM(tile_coef.shape, BF16),
            pltpu.VMEM((2,) + tile, BF16),
            pltpu.VMEM((n_blocks, half_c, rows_b), BF16),
            pltpu.VMEM((blocks, half_c, rows_b), F32),
            pltpu.VMEM((4,) + tile, F32),
            pltpu.VMEM((2,) + tile, BF16),
            pltpu.VMEM((blocks, half_c, rows_b), BF16),
            pltpu.VMEM((entries + 1, half_c, rows_b), F32),
            pltpu.VMEM((n2,) + tile, F32),
            pltpu.VMEM((n2,) + tile, F32),
            pltpu.VMEM((n2,) + tile, BF16),
            pltpu.VMEM((n2,) + tile, BF16),
            pltpu.VMEM((2, rows, cols), BF16),
            pltpu.VMEM((2, rows, cols), BF16),
            pltpu.VMEM((edges, cols), BF16),
            pltpu.VMEM((edges, cols), BF16),
            dma((7 + n_edge,)),
            dma((4,)),
            dma((4,)),
            dma((n2,)),
            dma((n2,)),
            dma((n2,)),
            dma((n2,)),
            dma((4,)),
            dma((4,)),
            dma((4,)),
            dma((4,)),
            dma(()),
            dma(()),
            dma((n2,)),
            dma((n2,)),
            dma((4,)),
            dma((4,)),
            dma((rows // span, 4)),
            dma((n_edge,)),
            dma((n_edge,)),
            dma((n_edge,)),
            dma(()),
        ],
        compiler_params=pltpu.CompilerParams(
            collective_id=0, has_side_effects=True, vmem_limit_bytes=40 * 1024 * 1024
        ),
        name="interaction",
    )(
        tile_source,
        links,
        wanted,
        w_bilinear,
        edge_embed,
        w_down,
        w_up,
        w_residual,
        tile_coef,
        cotangent,
    )


def silu_slope(value):
    sig = jax.nn.sigmoid(value)
    return sig * (1.0 + value * (1.0 - sig))


def feat_total(value):
    return lax.psum(value, "feat")


def rep_total(value):
    return lax.psum(value, "rep")


def trade(payload):
    return lax.all_to_all(payload, "edge", split_axis=0, concat_axis=0, tiled=True)


def contract(values, piece_weight):
    piece = lax.all_gather(values, "feat", axis=1, tiled=True)
    return jnp.dot(
        piece, piece_weight(jnp.int32(0), piece.shape[1]), preferred_element_type=jnp.float32
    )


def on_device(
    edge_embed, w_down, w_bilinear, w_up, w_residual, tile_coef, tile_source, target_rows, cotangent
):
    edges_dev, columns = edge_embed.shape
    blocks_dev, tiles_half, block_rows, _ = tile_coef.shape
    width_tri = w_down.shape[1]
    peers = lax.axis_size("edge")
    copies = lax.axis_size("rep")
    my_edge = lax.axis_index("edge")
    my_rep = lax.axis_index("rep")
    my_feat = lax.axis_index("feat")
    capacity = 2 * blocks_dev * tiles_half // peers
    entries = blocks_dev * tiles_half
    grid = tile_source.reshape(peers, blocks_dev, copies, tiles_half)
    lists = lax.dynamic_index_in_dim(grid, my_rep, axis=2, keepdims=False).reshape(peers, entries)
    owners = lists // blocks_dev
    local_ids = lists % blocks_dev
    hits = owners == my_edge
    slot_send = jnp.cumsum(hits.astype(jnp.int32), axis=1) - 1
    slot_range = jnp.arange(capacity, dtype=jnp.int32)
    picked = hits[:, :, None] & (slot_send[:, :, None] == slot_range[None, None, :])
    send_local = jnp.sum(jnp.where(picked, local_ids[:, :, None], 0), axis=1)
    send_valid = jnp.any(picked, axis=1)
    my_list = lax.dynamic_index_in_dim(lists, my_edge, 0, keepdims=False)
    my_owner = my_list // blocks_dev
    order = jnp.arange(entries, dtype=jnp.int32)
    same_before = (my_owner[:, None] == my_owner[None, :]) & (order[None, :] < order[:, None])
    my_slot = jnp.sum(same_before.astype(jnp.int32), axis=1)
    pre_down = feat_total(jnp.dot(edge_embed, w_down, preferred_element_type=jnp.float32))
    down_own = jax.nn.silu(pre_down).astype(jnp.bfloat16)
    down_blocks = down_own.reshape(blocks_dev, block_rows, width_tri)
    arrived = trade(down_blocks[send_local])
    sources = arrived[my_owner, my_slot]
    sources = sources.reshape(blocks_dev, tiles_half, block_rows, width_tri)
    partial_tri = jnp.einsum(
        "bkij,bkjc->bic", tile_coef, sources, preferred_element_type=jnp.float32
    )
    partial_tri = partial_tri.reshape(edges_dev, width_tri)
    tri_sum = rep_total(partial_tri).astype(jnp.bfloat16)
    pre_bil = jnp.dot(tri_sum, w_bilinear, preferred_element_type=jnp.float32)
    mid_act = jax.nn.silu(pre_bil).astype(jnp.bfloat16)
    hidden = (
        edge_embed.astype(jnp.float32) + jnp.dot(mid_act, w_up, preferred_element_type=jnp.float32)
    ).astype(jnp.bfloat16)
    saved = []
    for layer in range(w_residual.shape[0]):
        weight = w_residual[layer]

        def rows_piece(start, count, weight=weight):
            return lax.dynamic_slice(weight, (start, my_feat * columns), (count, columns))

        pre_res = contract(hidden, rows_piece)
        hidden = (hidden.astype(jnp.float32) + jax.nn.silu(pre_res)).astype(jnp.bfloat16)
        saved.append(pre_res)
    grad_hidden = cotangent.astype(jnp.float32)
    for layer in range(w_residual.shape[0] - 1, -1, -1):
        dz_layer = (grad_hidden * silu_slope(saved[layer])).astype(jnp.bfloat16)
        weight = w_residual[layer]

        def cols_piece(start, count, weight=weight):
            return lax.dynamic_slice(weight, (my_feat * columns, start), (columns, count)).T

        grad_hidden = grad_hidden + contract(dz_layer, cols_piece)
    grad_hb = grad_hidden.astype(jnp.bfloat16)
    grad_mid = feat_total(jnp.dot(grad_hb, w_up.T, preferred_element_type=jnp.float32))
    grad_bil = (grad_mid * silu_slope(pre_bil)).astype(jnp.bfloat16)
    grad_tri_own = jnp.dot(grad_bil, w_bilinear.T, preferred_element_type=jnp.float32).astype(
        jnp.bfloat16
    )
    grad_blocks = grad_tri_own.reshape(blocks_dev, block_rows, width_tri)
    contrib = jnp.einsum(
        "bkij,bic->bkjc", tile_coef, grad_blocks, preferred_element_type=jnp.float32
    ).astype(jnp.bfloat16)
    contrib = contrib.reshape(entries, block_rows, width_tri)
    outgoing = (
        jnp.zeros((peers, capacity, block_rows, width_tri), jnp.bfloat16)
        .at[my_owner, my_slot]
        .set(contrib)
    )
    incoming = trade(outgoing).reshape(peers * capacity, block_rows, width_tri)
    block_range = jnp.arange(blocks_dev, dtype=jnp.int32)
    select = (
        (send_local[:, :, None] == block_range[None, None, :]) & send_valid[:, :, None]
    ).astype(jnp.bfloat16)
    select = select.reshape(peers * capacity, blocks_dev)
    grad_down = jnp.einsum("sl,sjc->ljc", select, incoming, preferred_element_type=jnp.float32)
    grad_down = grad_down.reshape(edges_dev, width_tri)
    grad_down = rep_total(grad_down)
    grad_pre = (grad_down * silu_slope(pre_down)).astype(jnp.bfloat16)
    grad_edge = (
        grad_hb.astype(jnp.float32)
        + jnp.dot(grad_pre, w_down.T, preferred_element_type=jnp.float32)
    ).astype(jnp.bfloat16)
    span_rows = edges_dev // peers
    turned = lax.all_to_all(grad_edge, "edge", split_axis=0, concat_axis=0, tiled=True)
    position = target_rows // edges_dev * span_rows + target_rows % span_rows
    grad_target = turned[position]
    return (hidden, grad_target)


def solution(mesh):
    placed = (
        P(("grp", "edge"), "feat"),
        P("feat", None),
        P(),
        P(None, "feat"),
        P(),
        P(("grp", "edge"), "rep", None, None),
        P("grp", None),
        P(("grp", "edge")),
        P(("grp", "edge"), "feat"),
    )
    fits = mesh.shape["feat"] == 2 and mesh.shape["rep"] == 2
    return jax.shard_map(
        fused if fits else on_device,
        mesh=mesh,
        in_specs=placed,
        out_specs=(P(("grp", "edge"), "feat"), P(("grp", "edge"), "feat")),
        check_vma=False,
    )
```

```python
import functools

import jax
import jax.numpy as jnp
from jax import lax
from jax.experimental import pallas as pl
from jax.experimental.pallas import tpu as pltpu
from jax.sharding import PartitionSpec as P

MESH = pl.DeviceIdType.MESH
F32 = jnp.float32
BF16 = jnp.bfloat16


def mm(a, b, ca, cb):
    return lax.dot_general(a, b, (((ca,), (cb,)), ((), ())), preferred_element_type=F32)


def slope(value):
    sig = jax.nn.sigmoid(value)
    return sig * (1.0 + value * (1.0 - sig))


def block_kernel(
    n_edge,
    source,
    links,
    wanted_hbm,
    bil_hbm,
    edge_hbm,
    down_hbm,
    up_hbm,
    res_hbm,
    coef_hbm,
    cot_hbm,
    edge_out,
    grad_out,
    emb,
    emb_x,
    pd_part,
    pd_in,
    cot,
    wanted,
    w_bil,
    w_down,
    w_up,
    w_res,
    coef,
    down_mine,
    table,
    tri_part,
    tri_in,
    bil_mine,
    grad_tri,
    chain,
    pair_out,
    pair_in,
    red_out,
    red_in,
    out_mine,
    ge,
    turned,
    picks,
    hb_perm,
    gp_mine,
    gp_in,
    grad_v,
    local_sem,
    x_send,
    x_recv,
    tab_send,
    tab_recv,
    core_send,
    core_recv,
    tri_send,
    tri_recv,
    bil_send,
    bil_recv,
    pair_send,
    pair_recv,
    red_send,
    red_recv,
    out_send,
    out_recv,
    ge_send,
    ge_recv,
    fin_send,
    fin_recv,
    fin_local,
    gp_send,
    gp_recv,
):
    g = lax.axis_index("grp")
    e = lax.axis_index("edge")
    f = lax.axis_index("feat")
    r = lax.axis_index("rep")
    of = 1 - f
    orr = 1 - r
    s = 2 * f + r
    blocks, tiles, rows_b, _ = coef.shape
    bpd = blocks // 4
    rows = emb.shape[1]
    half_c = table.shape[1]
    span = turned.shape[0] // n_edge
    spd = rows // span
    hs = span // 2

    def peer(d, df, dr):
        return (g, lax.rem(e + d, n_edge), of if df else f, orr if dr else r)

    def remote(src, dst, ss, rs, dev):
        return pltpu.make_async_remote_copy(
            src_ref=src, dst_ref=dst, send_sem=ss, recv_sem=rs, device_id=dev, device_id_type=MESH
        )

    def mine(who):
        return pl.ds(who * rows, rows)

    partner_rows = mine(2 * of + r)
    local = [
        pltpu.make_async_copy(down_hbm, w_down, local_sem.at[0]),
        pltpu.make_async_copy(edge_hbm.at[mine(s)], emb.at[f], local_sem.at[1]),
        pltpu.make_async_copy(up_hbm, w_up.at[f], local_sem.at[2]),
        pltpu.make_async_copy(coef_hbm, coef, local_sem.at[3]),
        pltpu.make_async_copy(res_hbm, w_res, local_sem.at[4]),
        pltpu.make_async_copy(cot_hbm.at[mine(s)], cot.at[f], local_sem.at[5]),
        pltpu.make_async_copy(bil_hbm, w_bil, local_sem.at[7]),
        pltpu.make_async_copy(wanted_hbm, wanted, local_sem.at[8]),
        pltpu.make_async_copy(edge_hbm.at[partner_rows], emb_x, local_sem.at[9]),
    ]
    for copy in local:
        copy.start()

    barrier = pltpu.get_barrier_semaphore()
    others = 0
    for d in range(n_edge):
        for df in range(2):
            for dr in range(2):
                if d or df or dr:
                    pl.semaphore_signal(
                        barrier, inc=1, device_id=peer(d, df, dr), device_id_type=MESH
                    )
                    others += 1
    local[0].wait()
    local[1].wait()
    local[8].wait()
    wd = w_down[...]
    pd_part[...] = mm(wd, emb_x[...], 1, 1)
    own_part = mm(wd, emb[f], 1, 1)
    pl.semaphore_wait(barrier, others)

    across = peer(0, 1, 0)
    xs = [
        remote(pd_part, pd_in, x_send.at[0], x_recv.at[0], across),
        remote(emb_x, emb.at[f], x_send.at[1], x_recv.at[1], across),
        remote(up_hbm, w_up.at[f], x_send.at[2], x_recv.at[2], across),
        remote(cot_hbm.at[partner_rows], cot.at[f], x_send.at[3], x_recv.at[3], across),
    ]
    xs[0].start()
    xs[0].wait_recv()
    pre_down = own_part + pd_in[...]
    down = jax.nn.silu(pre_down).astype(BF16)
    for h in range(2):
        for b in range(bpd):
            down_mine[h, b] = down[h * half_c : (h + 1) * half_c, b * rows_b : (b + 1) * rows_b]

    def region(ed, who):
        return pl.ds(ed * blocks + who * bpd, bpd)

    tabs = []
    for i in range(1, 2 * n_edge):
        d, df = i // 2, i % 2
        copy = remote(
            down_mine.at[of if df else f],
            table.at[region(e, s)],
            tab_send.at[i],
            tab_recv.at[i],
            peer(d, df, 0),
        )
        copy.start()
        tabs.append(copy)
    own = remote(
        down_mine.at[f], table.at[region(e, s)], core_send.at[0], core_recv.at[0], peer(0, 0, 1)
    )
    own.start()
    xs[1].start()
    xs[2].start()
    table[region(e, s)] = down_mine[f]
    cores = [own]
    for i in range(1, 2 * n_edge):
        d, df = i // 2, i % 2
        tabs[i - 1].wait_recv()
        place = region(lax.rem(e + n_edge - d, n_edge), 2 * (of if df else f) + r)
        copy = remote(
            table.at[place], table.at[place], core_send.at[i], core_recv.at[i], peer(0, 0, 1)
        )
        copy.start()
        cores.append(copy)
    local[3].wait()
    for copy in cores:
        copy.wait_recv()

    xs[3].start()

    def forward(n, _):
        total = jnp.zeros((half_c, rows_b), F32)
        for k in range(tiles):
            total += mm(table[source[r * tiles + k, e * blocks + n]], coef[n, k], 1, 1)
        tri_part[n] = total
        return 0

    lax.fori_loop(0, blocks, forward, 0)
    tris = []
    for i in range(1, 4):
        df, dr = i // 2, i % 2
        to = 2 * (of if df else f) + (orr if dr else r)
        copy = remote(
            tri_part.at[pl.ds(to * bpd, bpd)],
            tri_in.at[i],
            tri_send.at[i],
            tri_recv.at[i],
            peer(0, df, dr),
        )
        copy.start()
        tris.append(copy)
    for copy in tris:
        copy.wait_recv()
    near = tri_part[pl.ds(s * bpd, bpd)] + tri_in[1]
    far = tri_in[2] + tri_in[3]
    low = jnp.where(f == 0, near, far)
    high = jnp.where(f == 0, far, near)
    tri = jnp.concatenate(
        [jnp.concatenate([low[b], high[b]], axis=0) for b in range(bpd)], axis=1
    ).astype(BF16)
    local[6].wait()
    wb = w_bil[...]
    pre_bil = mm(wb, tri, 0, 0)
    mid = jax.nn.silu(pre_bil).astype(BF16)
    local[2].wait()
    xs[2].wait_recv()
    xs[1].wait_recv()
    embed = jnp.concatenate([emb[0], emb[1]], axis=1)
    wu = jnp.concatenate([w_up[0], w_up[1]], axis=1)
    hidden = (embed.astype(F32) + mm(mid, wu, 0, 0)).astype(BF16)
    local[4].wait()
    saved = []
    for layer in range(w_res.shape[0]):
        pre = mm(hidden, w_res[layer], 1, 0)
        hidden = (hidden.astype(F32) + jax.nn.silu(pre)).astype(BF16)
        saved.append(slope(pre))
    cols = emb.shape[2]
    for h in range(2):
        out_mine[h] = hidden[:, h * cols : (h + 1) * cols]
    outs = []
    for i in range(1, 3):
        copy = remote(
            out_mine.at[of if i == 2 else f],
            edge_out.at[mine(s)],
            out_send.at[i],
            out_recv.at[i],
            peer(0, i // 2, i % 2),
        )
        copy.start()
        outs.append(copy)
    out_local = pltpu.make_async_copy(out_mine.at[f], edge_out.at[mine(s)], local_sem.at[6])
    out_local.start()
    local[5].wait()
    xs[3].wait_recv()
    grad = jnp.concatenate([cot[0], cot[1]], axis=1).astype(F32)
    for layer in range(w_res.shape[0] - 1, -1, -1):
        dz = (grad * saved[layer]).astype(BF16)
        grad = grad + mm(dz, w_res[layer], 1, 1)
    grad_hb = grad.astype(BF16)
    grad_bil = (mm(wu, grad_hb, 1, 1) * slope(pre_bil)).astype(BF16)
    grad_t = mm(wb, grad_bil, 1, 0).astype(BF16)
    for h in range(2):
        for b in range(bpd):
            bil_mine[h, b] = grad_t[h * half_c : (h + 1) * half_c, b * rows_b : (b + 1) * rows_b]
    bils = []
    for i in range(1, 4):
        df, dr = i // 2, i % 2
        copy = remote(
            bil_mine.at[of if df else f],
            grad_tri.at[pl.ds(s * bpd, bpd)],
            bil_send.at[i],
            bil_recv.at[i],
            peer(0, df, dr),
        )
        copy.start()
        bils.append(copy)
    for h in range(2):
        ge[h] = grad_hb[:, h * cols : (h + 1) * cols]
    sends = []
    for j in range(spd):
        q = s * spd + j
        d = lax.rem(q - e + n_edge, n_edge)
        for df in range(2):
            for dr in range(2):
                rt = orr if dr else r
                fr = of if df else f
                src = ge.at[fr, pl.ds(j * span + rt * hs, hs)]
                dst = turned.at[pl.ds(e * span + rt * hs, hs)]
                copy = remote(
                    src,
                    dst,
                    ge_send.at[j, 2 * df + dr],
                    ge_recv.at[d],
                    (g, q, fr, rt),
                )
                if df or dr:
                    copy.start()
                    sends.append((copy, None))
                else:
                    keep = pltpu.make_async_copy(src, dst, fin_local)

                    @pl.when(q == e)
                    def _(keep=keep):
                        keep.start()
                        keep.wait()

                    @pl.when(q != e)
                    def _(copy=copy):
                        copy.start()

                    sends.append((copy, q != e))
    grad_tri[pl.ds(s * bpd, bpd)] = bil_mine[f]
    chain[0] = jnp.zeros((half_c, rows_b), F32)
    for copy in bils:
        copy.wait_recv()

    def backward(n, _):
        block = grad_tri[n]
        parts = [mm(block, coef[n, k], 1, 0) for k in range(tiles)]
        for k in range(tiles):
            t = n * tiles + k
            chain[t + 1] = parts[k] + chain[links[t]]
        return 0

    lax.fori_loop(0, blocks, backward, 0)
    entries = blocks * tiles
    for i in range(2 * n_edge):
        for b in range(bpd):
            block_id = (i // 2) * blocks + (2 * (i % 2) + orr) * bpd + b
            pair_out[i, b] = chain[links[entries + block_id]]
    pair = remote(pair_out, pair_in, pair_send, pair_recv, peer(0, 0, 1))
    pair.start()
    pair.wait_recv()
    for i in range(2 * n_edge):
        for b in range(bpd):
            block_id = (i // 2) * blocks + (2 * (i % 2) + r) * bpd + b
            red_out[i, b] = (chain[links[entries + block_id]] + pair_in[i, b]).astype(BF16)
    reds = []
    for i in range(1, 2 * n_edge):
        d, df = i // 2, i % 2
        slot = 2 * lax.rem(e + d, n_edge) + (of if df else f)
        copy = remote(
            red_out.at[slot], red_in.at[i], red_send.at[i], red_recv.at[i], peer(d, df, 0)
        )
        copy.start()
        reds.append(copy)
    fins = []
    for d in range(n_edge):
        p = lax.rem(e + n_edge - d, n_edge)
        place = pl.ds(p * span + r * hs, hs)
        arrive = remote(
            turned.at[place], turned.at[place], ge_send.at[0, 0], ge_recv.at[d], peer(0, 0, 1)
        )
        if d:
            arrive.wait_recv()
        else:

            @pl.when(s != e // spd)
            def _(arrive=arrive):
                arrive.wait_recv()

        copy = remote(
            turned.at[place], turned.at[place], fin_send.at[d], fin_recv.at[d], peer(0, 0, 1)
        )
        copy.start()
        fins.append(copy)
    relay_rows = mine(2 * of + r)
    outs[1].wait_recv()
    relay = remote(
        edge_out.at[relay_rows], edge_out.at[relay_rows], out_send.at[3], out_recv.at[3], peer(0, 0, 1)
    )
    relay.start()
    for copy in reds:
        copy.wait_recv()
    near = red_out[2 * e + f].astype(F32)
    far = red_in[1].astype(F32)
    for d in range(1, n_edge):
        near += red_in[2 * d].astype(F32)
        far += red_in[2 * d + 1].astype(F32)
    low = jnp.where(f == 0, near, far)
    high = jnp.where(f == 0, far, near)
    grad_down = jnp.concatenate(
        [jnp.concatenate([low[b], high[b]], axis=0) for b in range(bpd)], axis=1
    )
    grad_pre = (grad_down * slope(pre_down)).astype(BF16)
    given = []
    for j in range(spd):
        gp_mine[j] = grad_pre[:, j * span : (j + 1) * span]
        q = s * spd + j
        d = lax.rem(q - e + n_edge, n_edge)
        for df in range(2):
            for dr in range(2):
                copy = remote(
                    gp_mine.at[j],
                    gp_in.at[e],
                    gp_send.at[j, 2 * df + dr],
                    gp_recv.at[d],
                    (g, q, of if df else f, orr if dr else r),
                )
                if df or dr:
                    copy.start()
                    given.append((copy, None))
                else:

                    @pl.when(q == e)
                    def _(j=j):
                        gp_in[e] = gp_mine[j]

                    @pl.when(q != e)
                    def _(copy=copy):
                        copy.start()

                    given.append((copy, q != e))
    local[7].wait()
    for d in range(n_edge):
        p = lax.rem(e + n_edge - d, n_edge)
        fins[d].wait_recv()
        wish = wanted[p] - (p * turned.shape[0] + e * span)
        slot = lax.broadcasted_iota(jnp.int32, (span, span), 0)
        pick = jnp.where(slot == wish, 1.0, 0.0).astype(BF16)
        picks[d] = pick
        hb_perm[d] = mm(pick, turned[pl.ds(p * span, span)], 0, 0).astype(BF16)
    writes = []
    for d in range(n_edge):
        p = lax.rem(e + n_edge - d, n_edge)
        arrive = remote(gp_mine.at[0], gp_in.at[p], gp_send.at[0, 0], gp_recv.at[d], peer(0, 0, 1))
        if d:
            arrive.wait_recv()
        else:

            @pl.when(s != e // spd)
            def _(arrive=arrive):
                arrive.wait_recv()

        moved = mm(gp_in[p], picks[d], 1, 0).astype(BF16)
        place = pl.ds(p * span, span)
        grad_v[place] = (hb_perm[d].astype(F32) + mm(moved, wd, 0, 0)).astype(BF16)
        copy = pltpu.make_async_copy(grad_v.at[place], grad_out.at[place], local_sem.at[10 + d])
        copy.start()
        writes.append(copy)
    relay.wait_recv()
    outs[0].wait_recv()
    out_local.wait()
    for copy in xs + tabs + cores + tris + outs + [relay] + bils + [pair] + reds + fins:
        copy.wait_send()
    for copy, when in sends + given:
        if when is None:
            copy.wait_send()
        else:

            @pl.when(when)
            def _(copy=copy):
                copy.wait_send()

    for copy in writes:
        copy.wait()


def fused(
    edge_embed, w_down, w_bilinear, w_up, w_residual, tile_coef, tile_source, target_rows, cotangent
):
    n_edge = lax.axis_size("edge")
    edges, cols = edge_embed.shape
    blocks, tiles, rows_b, _ = tile_coef.shape
    width = w_down.shape[1]
    half_c = width // 2
    bpd = blocks // 4
    rows = edges // 4
    span = edges // n_edge
    n_blocks = n_edge * blocks
    entries = blocks * tiles
    mine = lax.dynamic_slice(
        tile_source,
        (lax.axis_index("edge") * blocks, lax.axis_index("rep") * tiles),
        (blocks, tiles),
    ).reshape(entries)
    asked = jnp.concatenate([mine, jnp.arange(n_blocks, dtype=jnp.int32)])
    before = jnp.concatenate(
        [jnp.arange(entries, dtype=jnp.int32), jnp.full((n_blocks,), entries, jnp.int32)]
    )
    order = jnp.arange(entries, dtype=jnp.int32)
    same = (asked[:, None] == mine[None, :]) & (order[None, :] < before[:, None])
    links = jnp.max(jnp.where(same, order[None, :] + 1, 0), axis=1)
    wanted = target_rows.reshape(n_edge, 1, span)
    smem = pl.BlockSpec(memory_space=pltpu.SMEM)
    hbm = pl.BlockSpec(memory_space=pl.ANY)
    dma = pltpu.SemaphoreType.DMA
    tile = (bpd, half_c, rows_b)
    n2 = 2 * n_edge
    return pl.pallas_call(
        functools.partial(block_kernel, n_edge),
        out_shape=[jax.ShapeDtypeStruct((edges, cols), BF16)] * 2,
        in_specs=[smem, smem] + [hbm] * 8,
        out_specs=[hbm, hbm],
        scratch_shapes=[
            pltpu.VMEM((2, rows, cols), BF16),
            pltpu.VMEM((rows, cols), BF16),
            pltpu.VMEM((width, rows), F32),
            pltpu.VMEM((width, rows), F32),
            pltpu.VMEM((2, rows, cols), BF16),
            pltpu.VMEM(wanted.shape, jnp.int32),
            pltpu.VMEM(w_bilinear.shape, BF16),
            pltpu.VMEM(w_down.shape[::-1], BF16),
            pltpu.VMEM((2,) + w_up.shape, BF16),
            pltpu.VMEM(w_residual.shape, BF16),
            pltpu.VMEM(tile_coef.shape, BF16),
            pltpu.VMEM((2,) + tile, BF16),
            pltpu.VMEM((n_blocks, half_c, rows_b), BF16),
            pltpu.VMEM((blocks, half_c, rows_b), F32),
            pltpu.VMEM((4,) + tile, F32),
            pltpu.VMEM((2,) + tile, BF16),
            pltpu.VMEM((blocks, half_c, rows_b), BF16),
            pltpu.VMEM((entries + 1, half_c, rows_b), F32),
            pltpu.VMEM((n2,) + tile, F32),
            pltpu.VMEM((n2,) + tile, F32),
            pltpu.VMEM((n2,) + tile, BF16),
            pltpu.VMEM((n2,) + tile, BF16),
            pltpu.VMEM((2, rows, cols), BF16),
            pltpu.VMEM((2, rows, cols), BF16),
            pltpu.VMEM((edges, cols), BF16),
            pltpu.VMEM((n_edge, span, span), BF16),
            pltpu.VMEM((n_edge, span, cols), BF16),
            pltpu.VMEM((rows // span, width, span), BF16),
            pltpu.VMEM((n_edge, width, span), BF16),
            pltpu.VMEM((edges, cols), BF16),
            dma((10 + n_edge,)),
            dma((4,)),
            dma((4,)),
            dma((n2,)),
            dma((n2,)),
            dma((n2,)),
            dma((n2,)),
            dma((4,)),
            dma((4,)),
            dma((4,)),
            dma((4,)),
            dma(()),
            dma(()),
            dma((n2,)),
            dma((n2,)),
            dma((4,)),
            dma((4,)),
            dma((rows // span, 4)),
            dma((n_edge,)),
            dma((n_edge,)),
            dma((n_edge,)),
            dma(()),
            dma((rows // span, 4)),
            dma((n_edge,)),
        ],
        compiler_params=pltpu.CompilerParams(
            collective_id=0, has_side_effects=True, vmem_limit_bytes=62 * 1024 * 1024
        ),
        name="interaction",
    )(
        tile_source.T,
        links,
        wanted,
        w_bilinear,
        edge_embed,
        w_down.T,
        w_up,
        w_residual,
        tile_coef,
        cotangent,
    )


def silu_slope(value):
    sig = jax.nn.sigmoid(value)
    return sig * (1.0 + value * (1.0 - sig))


def feat_total(value):
    return lax.psum(value, "feat")


def rep_total(value):
    return lax.psum(value, "rep")


def trade(payload):
    return lax.all_to_all(payload, "edge", split_axis=0, concat_axis=0, tiled=True)


def contract(values, piece_weight):
    piece = lax.all_gather(values, "feat", axis=1, tiled=True)
    return jnp.dot(
        piece, piece_weight(jnp.int32(0), piece.shape[1]), preferred_element_type=jnp.float32
    )


def on_device(
    edge_embed, w_down, w_bilinear, w_up, w_residual, tile_coef, tile_source, target_rows, cotangent
):
    edges_dev, columns = edge_embed.shape
    blocks_dev, tiles_half, block_rows, _ = tile_coef.shape
    width_tri = w_down.shape[1]
    peers = lax.axis_size("edge")
    copies = lax.axis_size("rep")
    my_edge = lax.axis_index("edge")
    my_rep = lax.axis_index("rep")
    my_feat = lax.axis_index("feat")
    capacity = 2 * blocks_dev * tiles_half // peers
    entries = blocks_dev * tiles_half
    grid = tile_source.reshape(peers, blocks_dev, copies, tiles_half)
    lists = lax.dynamic_index_in_dim(grid, my_rep, axis=2, keepdims=False).reshape(peers, entries)
    owners = lists // blocks_dev
    local_ids = lists % blocks_dev
    hits = owners == my_edge
    slot_send = jnp.cumsum(hits.astype(jnp.int32), axis=1) - 1
    slot_range = jnp.arange(capacity, dtype=jnp.int32)
    picked = hits[:, :, None] & (slot_send[:, :, None] == slot_range[None, None, :])
    send_local = jnp.sum(jnp.where(picked, local_ids[:, :, None], 0), axis=1)
    send_valid = jnp.any(picked, axis=1)
    my_list = lax.dynamic_index_in_dim(lists, my_edge, 0, keepdims=False)
    my_owner = my_list // blocks_dev
    order = jnp.arange(entries, dtype=jnp.int32)
    same_before = (my_owner[:, None] == my_owner[None, :]) & (order[None, :] < order[:, None])
    my_slot = jnp.sum(same_before.astype(jnp.int32), axis=1)
    pre_down = feat_total(jnp.dot(edge_embed, w_down, preferred_element_type=jnp.float32))
    down_own = jax.nn.silu(pre_down).astype(jnp.bfloat16)
    down_blocks = down_own.reshape(blocks_dev, block_rows, width_tri)
    arrived = trade(down_blocks[send_local])
    sources = arrived[my_owner, my_slot]
    sources = sources.reshape(blocks_dev, tiles_half, block_rows, width_tri)
    partial_tri = jnp.einsum(
        "bkij,bkjc->bic", tile_coef, sources, preferred_element_type=jnp.float32
    )
    partial_tri = partial_tri.reshape(edges_dev, width_tri)
    tri_sum = rep_total(partial_tri).astype(jnp.bfloat16)
    pre_bil = jnp.dot(tri_sum, w_bilinear, preferred_element_type=jnp.float32)
    mid_act = jax.nn.silu(pre_bil).astype(jnp.bfloat16)
    hidden = (
        edge_embed.astype(jnp.float32) + jnp.dot(mid_act, w_up, preferred_element_type=jnp.float32)
    ).astype(jnp.bfloat16)
    saved = []
    for layer in range(w_residual.shape[0]):
        weight = w_residual[layer]

        def rows_piece(start, count, weight=weight):
            return lax.dynamic_slice(weight, (start, my_feat * columns), (count, columns))

        pre_res = contract(hidden, rows_piece)
        hidden = (hidden.astype(jnp.float32) + jax.nn.silu(pre_res)).astype(jnp.bfloat16)
        saved.append(pre_res)
    grad_hidden = cotangent.astype(jnp.float32)
    for layer in range(w_residual.shape[0] - 1, -1, -1):
        dz_layer = (grad_hidden * silu_slope(saved[layer])).astype(jnp.bfloat16)
        weight = w_residual[layer]

        def cols_piece(start, count, weight=weight):
            return lax.dynamic_slice(weight, (my_feat * columns, start), (columns, count)).T

        grad_hidden = grad_hidden + contract(dz_layer, cols_piece)
    grad_hb = grad_hidden.astype(jnp.bfloat16)
    grad_mid = feat_total(jnp.dot(grad_hb, w_up.T, preferred_element_type=jnp.float32))
    grad_bil = (grad_mid * silu_slope(pre_bil)).astype(jnp.bfloat16)
    grad_tri_own = jnp.dot(grad_bil, w_bilinear.T, preferred_element_type=jnp.float32).astype(
        jnp.bfloat16
    )
    grad_blocks = grad_tri_own.reshape(blocks_dev, block_rows, width_tri)
    contrib = jnp.einsum(
        "bkij,bic->bkjc", tile_coef, grad_blocks, preferred_element_type=jnp.float32
    ).astype(jnp.bfloat16)
    contrib = contrib.reshape(entries, block_rows, width_tri)
    outgoing = (
        jnp.zeros((peers, capacity, block_rows, width_tri), jnp.bfloat16)
        .at[my_owner, my_slot]
        .set(contrib)
    )
    incoming = trade(outgoing).reshape(peers * capacity, block_rows, width_tri)
    block_range = jnp.arange(blocks_dev, dtype=jnp.int32)
    select = (
        (send_local[:, :, None] == block_range[None, None, :]) & send_valid[:, :, None]
    ).astype(jnp.bfloat16)
    select = select.reshape(peers * capacity, blocks_dev)
    grad_down = jnp.einsum("sl,sjc->ljc", select, incoming, preferred_element_type=jnp.float32)
    grad_down = grad_down.reshape(edges_dev, width_tri)
    grad_down = rep_total(grad_down)
    grad_pre = (grad_down * silu_slope(pre_down)).astype(jnp.bfloat16)
    grad_edge = (
        grad_hb.astype(jnp.float32)
        + jnp.dot(grad_pre, w_down.T, preferred_element_type=jnp.float32)
    ).astype(jnp.bfloat16)
    span_rows = edges_dev // peers
    turned = lax.all_to_all(grad_edge, "edge", split_axis=0, concat_axis=0, tiled=True)
    position = target_rows // edges_dev * span_rows + target_rows % span_rows
    grad_target = turned[position]
    return (hidden, grad_target)


def solution(mesh):
    placed = (
        P(("grp", "edge"), "feat"),
        P("feat", None),
        P(),
        P(None, "feat"),
        P(),
        P(("grp", "edge"), "rep", None, None),
        P("grp", None),
        P(("grp", "edge")),
        P(("grp", "edge"), "feat"),
    )
    fits = mesh.shape["feat"] == 2 and mesh.shape["rep"] == 2 and mesh.shape["edge"] in (4, 8)
    return jax.shard_map(
        fused if fits else on_device,
        mesh=mesh,
        in_specs=placed,
        out_specs=(P(("grp", "edge"), "feat"), P(("grp", "edge"), "feat")),
        check_vma=False,
    )
```

```python
import functools

import jax
import jax.numpy as jnp
from jax import lax
from jax.experimental import pallas as pl
from jax.experimental.pallas import tpu as pltpu
from jax.sharding import PartitionSpec as P

MESH = pl.DeviceIdType.MESH
F32 = jnp.float32
BF16 = jnp.bfloat16


def mm(a, b, ca, cb):
    return lax.dot_general(a, b, (((ca,), (cb,)), ((), ())), preferred_element_type=F32)


def slope(value):
    sig = jax.nn.sigmoid(value)
    return sig * (1.0 + value * (1.0 - sig))


def block_kernel(
    n_edge,
    source_hbm,
    wanted_hbm,
    bil_hbm,
    edge_hbm,
    down_hbm,
    up_hbm,
    res_hbm,
    coef_hbm,
    cot_hbm,
    edge_out,
    grad_out,
    emb,
    emb_x,
    pd_part,
    pd_in,
    cot,
    wanted,
    w_bil,
    w_down,
    w_up,
    w_res,
    coef,
    down_mine,
    table,
    tri_part,
    tri_in,
    bil_mine,
    grad_tri,
    chain,
    pair_out,
    pair_in,
    red_out,
    red_in,
    out_mine,
    ge,
    turned,
    picks,
    hb_perm,
    source,
    seen,
    newest,
    before,
    last,
    gp_mine,
    gp_in,
    grad_v,
    local_sem,
    x_send,
    x_recv,
    tab_send,
    tab_recv,
    core_send,
    core_recv,
    tri_send,
    tri_recv,
    bil_send,
    bil_recv,
    pair_send,
    pair_recv,
    red_send,
    red_recv,
    out_send,
    out_recv,
    ge_send,
    ge_recv,
    fin_send,
    fin_recv,
    fin_local,
    gp_send,
    gp_recv,
):
    g = lax.axis_index("grp")
    e = lax.axis_index("edge")
    f = lax.axis_index("feat")
    r = lax.axis_index("rep")
    of = 1 - f
    orr = 1 - r
    s = 2 * f + r
    blocks, tiles, rows_b, _ = coef.shape
    bpd = blocks // 4
    rows = emb.shape[1]
    half_c = table.shape[1]
    span = turned.shape[0] // n_edge
    spd = rows // span
    hs = span // 2

    def peer(d, df, dr):
        return (g, lax.rem(e + d, n_edge), of if df else f, orr if dr else r)

    def remote(src, dst, ss, rs, dev):
        return pltpu.make_async_remote_copy(
            src_ref=src, dst_ref=dst, send_sem=ss, recv_sem=rs, device_id=dev, device_id_type=MESH
        )

    def mine(who):
        return pl.ds(who * rows, rows)

    partner_rows = mine(2 * of + r)
    local = [
        pltpu.make_async_copy(down_hbm, w_down, local_sem.at[0]),
        pltpu.make_async_copy(edge_hbm.at[mine(s)], emb.at[f], local_sem.at[1]),
        pltpu.make_async_copy(up_hbm, w_up.at[f], local_sem.at[2]),
        pltpu.make_async_copy(coef_hbm, coef, local_sem.at[3]),
        pltpu.make_async_copy(res_hbm, w_res, local_sem.at[4]),
        pltpu.make_async_copy(cot_hbm.at[mine(s)], cot.at[f], local_sem.at[5]),
        pltpu.make_async_copy(bil_hbm, w_bil, local_sem.at[7]),
        pltpu.make_async_copy(wanted_hbm, wanted, local_sem.at[8]),
        pltpu.make_async_copy(edge_hbm.at[partner_rows], emb_x, local_sem.at[9]),
        pltpu.make_async_copy(source_hbm, source, local_sem.at[10]),
    ]
    for copy in local:
        copy.start()

    barrier = pltpu.get_barrier_semaphore()
    others = 0
    for d in range(n_edge):
        for df in range(2):
            for dr in range(2):
                if d or df or dr:
                    pl.semaphore_signal(
                        barrier, inc=1, device_id=peer(d, df, dr), device_id_type=MESH
                    )
                    others += 1
    local[0].wait()
    local[1].wait()
    local[8].wait()
    wd = w_down[...]
    pd_part[...] = mm(wd, emb_x[...], 1, 1)
    own_part = mm(wd, emb[f], 1, 1)
    pl.semaphore_wait(barrier, others)

    across = peer(0, 1, 0)
    xs = [
        remote(pd_part, pd_in, x_send.at[0], x_recv.at[0], across),
        remote(emb_x, emb.at[f], x_send.at[1], x_recv.at[1], across),
        remote(up_hbm, w_up.at[f], x_send.at[2], x_recv.at[2], across),
        remote(cot_hbm.at[partner_rows], cot.at[f], x_send.at[3], x_recv.at[3], across),
    ]
    xs[0].start()
    xs[0].wait_recv()
    pre_down = own_part + pd_in[...]
    down = jax.nn.silu(pre_down).astype(BF16)
    for h in range(2):
        for b in range(bpd):
            down_mine[h, b] = down[h * half_c : (h + 1) * half_c, b * rows_b : (b + 1) * rows_b]

    def region(ed, who):
        return pl.ds(ed * blocks + who * bpd, bpd)

    tabs = []
    for i in range(1, 2 * n_edge):
        d, df = i // 2, i % 2
        copy = remote(
            down_mine.at[of if df else f],
            table.at[region(e, s)],
            tab_send.at[i],
            tab_recv.at[i],
            peer(d, df, 0),
        )
        copy.start()
        tabs.append(copy)
    own = remote(
        down_mine.at[f], table.at[region(e, s)], core_send.at[0], core_recv.at[0], peer(0, 0, 1)
    )
    own.start()
    xs[1].start()
    xs[2].start()
    table[region(e, s)] = down_mine[f]
    local[9].wait()
    entries = blocks * tiles
    lanes = newest.shape[1]
    ids = lax.broadcasted_iota(jnp.int32, (1, lanes), 1)
    latest = jnp.zeros((1, lanes), jnp.int32)
    for t in range(entries):
        hit = ids == source[r * tiles + t % tiles, e * blocks + t // tiles]
        seen[t : t + 1, :] = jnp.where(hit, latest, 0)
        latest = jnp.where(hit, t + 1, latest)
    newest[...] = latest
    seen[...] = jnp.broadcast_to(jnp.max(seen[...], axis=1, keepdims=True), seen.shape)
    lists = [
        pltpu.make_async_copy(seen, before, local_sem.at[11]),
        pltpu.make_async_copy(newest, last, local_sem.at[12]),
    ]
    for copy in lists:
        copy.start()
    cores = [own]
    for i in range(1, 2 * n_edge):
        d, df = i // 2, i % 2
        tabs[i - 1].wait_recv()
        place = region(lax.rem(e + n_edge - d, n_edge), 2 * (of if df else f) + r)
        copy = remote(
            table.at[place], table.at[place], core_send.at[i], core_recv.at[i], peer(0, 0, 1)
        )
        copy.start()
        cores.append(copy)
    local[3].wait()
    for copy in cores:
        copy.wait_recv()

    xs[3].start()

    def forward(n, _):
        total = jnp.zeros((half_c, rows_b), F32)
        for k in range(tiles):
            total += mm(table[source[r * tiles + k, e * blocks + n]], coef[n, k], 1, 1)
        tri_part[n] = total
        return 0

    lax.fori_loop(0, blocks, forward, 0)
    tris = []
    for i in range(1, 4):
        df, dr = i // 2, i % 2
        to = 2 * (of if df else f) + (orr if dr else r)
        copy = remote(
            tri_part.at[pl.ds(to * bpd, bpd)],
            tri_in.at[i],
            tri_send.at[i],
            tri_recv.at[i],
            peer(0, df, dr),
        )
        copy.start()
        tris.append(copy)
    for copy in tris:
        copy.wait_recv()
    near = tri_part[pl.ds(s * bpd, bpd)] + tri_in[1]
    far = tri_in[2] + tri_in[3]
    low = jnp.where(f == 0, near, far)
    high = jnp.where(f == 0, far, near)
    tri = jnp.concatenate(
        [jnp.concatenate([low[b], high[b]], axis=0) for b in range(bpd)], axis=1
    ).astype(BF16)
    local[6].wait()
    wb = w_bil[...]
    pre_bil = mm(wb, tri, 0, 0)
    mid = jax.nn.silu(pre_bil).astype(BF16)
    local[2].wait()
    xs[2].wait_recv()
    xs[1].wait_recv()
    embed = jnp.concatenate([emb[0], emb[1]], axis=1)
    wu = jnp.concatenate([w_up[0], w_up[1]], axis=1)
    hidden = (embed.astype(F32) + mm(mid, wu, 0, 0)).astype(BF16)
    local[4].wait()
    saved = []
    for layer in range(w_res.shape[0]):
        pre = mm(hidden, w_res[layer], 1, 0)
        hidden = (hidden.astype(F32) + jax.nn.silu(pre)).astype(BF16)
        saved.append(slope(pre))
    cols = emb.shape[2]
    for h in range(2):
        out_mine[h] = hidden[:, h * cols : (h + 1) * cols]
    outs = []
    for i in range(1, 3):
        copy = remote(
            out_mine.at[of if i == 2 else f],
            edge_out.at[mine(s)],
            out_send.at[i],
            out_recv.at[i],
            peer(0, i // 2, i % 2),
        )
        copy.start()
        outs.append(copy)
    out_local = pltpu.make_async_copy(out_mine.at[f], edge_out.at[mine(s)], local_sem.at[6])
    out_local.start()
    local[5].wait()
    xs[3].wait_recv()
    grad = jnp.concatenate([cot[0], cot[1]], axis=1).astype(F32)
    for layer in range(w_res.shape[0] - 1, -1, -1):
        dz = (grad * saved[layer]).astype(BF16)
        grad = grad + mm(dz, w_res[layer], 1, 1)
    grad_hb = grad.astype(BF16)
    grad_bil = (mm(wu, grad_hb, 1, 1) * slope(pre_bil)).astype(BF16)
    grad_t = mm(wb, grad_bil, 1, 0).astype(BF16)
    for h in range(2):
        for b in range(bpd):
            bil_mine[h, b] = grad_t[h * half_c : (h + 1) * half_c, b * rows_b : (b + 1) * rows_b]
    bils = []
    for i in range(1, 4):
        df, dr = i // 2, i % 2
        copy = remote(
            bil_mine.at[of if df else f],
            grad_tri.at[pl.ds(s * bpd, bpd)],
            bil_send.at[i],
            bil_recv.at[i],
            peer(0, df, dr),
        )
        copy.start()
        bils.append(copy)
    for h in range(2):
        ge[h] = grad_hb[:, h * cols : (h + 1) * cols]
    sends = []
    for j in range(spd):
        q = s * spd + j
        d = lax.rem(q - e + n_edge, n_edge)
        for df in range(2):
            for dr in range(2):
                rt = orr if dr else r
                fr = of if df else f
                src = ge.at[fr, pl.ds(j * span + rt * hs, hs)]
                dst = turned.at[pl.ds(e * span + rt * hs, hs)]
                copy = remote(
                    src,
                    dst,
                    ge_send.at[j, 2 * df + dr],
                    ge_recv.at[d],
                    (g, q, fr, rt),
                )
                if df or dr:
                    copy.start()
                    sends.append((copy, None))
                else:
                    keep = pltpu.make_async_copy(src, dst, fin_local)

                    @pl.when(q == e)
                    def _(keep=keep):
                        keep.start()
                        keep.wait()

                    @pl.when(q != e)
                    def _(copy=copy):
                        copy.start()

                    sends.append((copy, q != e))
    grad_tri[pl.ds(s * bpd, bpd)] = bil_mine[f]
    chain[0] = jnp.zeros((half_c, rows_b), F32)
    for copy in lists:
        copy.wait()
    for copy in bils:
        copy.wait_recv()

    def backward(n, _):
        block = grad_tri[n]
        parts = [mm(block, coef[n, k], 1, 0) for k in range(tiles)]
        for k in range(tiles):
            t = n * tiles + k
            chain[t + 1] = parts[k] + chain[before[t, 0]]
        return 0

    lax.fori_loop(0, blocks, backward, 0)
    for i in range(2 * n_edge):
        for b in range(bpd):
            block_id = (i // 2) * blocks + (2 * (i % 2) + orr) * bpd + b
            pair_out[i, b] = chain[last[0, block_id]]
    pair = remote(pair_out, pair_in, pair_send, pair_recv, peer(0, 0, 1))
    pair.start()
    pair.wait_recv()
    for i in range(2 * n_edge):
        for b in range(bpd):
            block_id = (i // 2) * blocks + (2 * (i % 2) + r) * bpd + b
            red_out[i, b] = (chain[last[0, block_id]] + pair_in[i, b]).astype(BF16)
    reds = []
    for i in range(1, 2 * n_edge):
        d, df = i // 2, i % 2
        slot = 2 * lax.rem(e + d, n_edge) + (of if df else f)
        copy = remote(
            red_out.at[slot], red_in.at[i], red_send.at[i], red_recv.at[i], peer(d, df, 0)
        )
        copy.start()
        reds.append(copy)
    fins = []
    for d in range(n_edge):
        p = lax.rem(e + n_edge - d, n_edge)
        place = pl.ds(p * span + r * hs, hs)
        arrive = remote(
            turned.at[place], turned.at[place], ge_send.at[0, 0], ge_recv.at[d], peer(0, 0, 1)
        )
        if d:
            arrive.wait_recv()
        else:

            @pl.when(s != e // spd)
            def _(arrive=arrive):
                arrive.wait_recv()

        copy = remote(
            turned.at[place], turned.at[place], fin_send.at[d], fin_recv.at[d], peer(0, 0, 1)
        )
        copy.start()
        fins.append(copy)
    relay_rows = mine(2 * of + r)
    outs[1].wait_recv()
    relay = remote(
        edge_out.at[relay_rows], edge_out.at[relay_rows], out_send.at[3], out_recv.at[3], peer(0, 0, 1)
    )
    relay.start()
    for copy in reds:
        copy.wait_recv()
    near = red_out[2 * e + f].astype(F32)
    far = red_in[1].astype(F32)
    for d in range(1, n_edge):
        near += red_in[2 * d].astype(F32)
        far += red_in[2 * d + 1].astype(F32)
    low = jnp.where(f == 0, near, far)
    high = jnp.where(f == 0, far, near)
    grad_down = jnp.concatenate(
        [jnp.concatenate([low[b], high[b]], axis=0) for b in range(bpd)], axis=1
    )
    grad_pre = (grad_down * slope(pre_down)).astype(BF16)
    given = []
    for j in range(spd):
        gp_mine[j] = grad_pre[:, j * span : (j + 1) * span]
        q = s * spd + j
        d = lax.rem(q - e + n_edge, n_edge)
        for df in range(2):
            for dr in range(2):
                copy = remote(
                    gp_mine.at[j],
                    gp_in.at[e],
                    gp_send.at[j, 2 * df + dr],
                    gp_recv.at[d],
                    (g, q, of if df else f, orr if dr else r),
                )
                if df or dr:
                    copy.start()
                    given.append((copy, None))
                else:

                    @pl.when(q == e)
                    def _(j=j):
                        gp_in[e] = gp_mine[j]

                    @pl.when(q != e)
                    def _(copy=copy):
                        copy.start()

                    given.append((copy, q != e))
    local[7].wait()
    for d in range(n_edge):
        p = lax.rem(e + n_edge - d, n_edge)
        fins[d].wait_recv()
        wish = wanted[p] - (p * turned.shape[0] + e * span)
        slot = lax.broadcasted_iota(jnp.int32, (span, span), 0)
        pick = jnp.where(slot == wish, 1.0, 0.0).astype(BF16)
        picks[d] = pick
        hb_perm[d] = mm(pick, turned[pl.ds(p * span, span)], 0, 0).astype(BF16)
    writes = []
    for d in range(n_edge):
        p = lax.rem(e + n_edge - d, n_edge)
        arrive = remote(gp_mine.at[0], gp_in.at[p], gp_send.at[0, 0], gp_recv.at[d], peer(0, 0, 1))
        if d:
            arrive.wait_recv()
        else:

            @pl.when(s != e // spd)
            def _(arrive=arrive):
                arrive.wait_recv()

        moved = mm(gp_in[p], picks[d], 1, 0).astype(BF16)
        place = pl.ds(p * span, span)
        grad_v[place] = (hb_perm[d].astype(F32) + mm(moved, wd, 0, 0)).astype(BF16)
        copy = pltpu.make_async_copy(grad_v.at[place], grad_out.at[place], local_sem.at[13 + d])
        copy.start()
        writes.append(copy)
    relay.wait_recv()
    outs[0].wait_recv()
    out_local.wait()
    for copy in xs + tabs + cores + tris + outs + [relay] + bils + [pair] + reds + fins:
        copy.wait_send()
    for copy, when in sends + given:
        if when is None:
            copy.wait_send()
        else:

            @pl.when(when)
            def _(copy=copy):
                copy.wait_send()

    for copy in writes:
        copy.wait()


def fused(
    edge_embed, w_down, w_bilinear, w_up, w_residual, tile_coef, tile_source, target_rows, cotangent
):
    n_edge = lax.axis_size("edge")
    edges, cols = edge_embed.shape
    blocks, tiles, rows_b, _ = tile_coef.shape
    width = w_down.shape[1]
    half_c = width // 2
    bpd = blocks // 4
    rows = edges // 4
    span = edges // n_edge
    n_blocks = n_edge * blocks
    entries = blocks * tiles
    lanes = -(-n_blocks // 128) * 128
    wanted = target_rows.reshape(n_edge, 1, span)
    fixed = pl.BlockSpec(memory_space=pltpu.HBM)
    hbm = pl.BlockSpec(memory_space=pl.ANY)
    dma = pltpu.SemaphoreType.DMA
    tile = (bpd, half_c, rows_b)
    n2 = 2 * n_edge
    return pl.pallas_call(
        functools.partial(block_kernel, n_edge),
        out_shape=[pltpu.VMEM((edges, cols), BF16)] * 2,
        in_specs=[fixed] * 9,
        out_specs=[hbm, hbm],
        scratch_shapes=[
            pltpu.VMEM((2, rows, cols), BF16),
            pltpu.VMEM((rows, cols), BF16),
            pltpu.VMEM((width, rows), F32),
            pltpu.VMEM((width, rows), F32),
            pltpu.VMEM((2, rows, cols), BF16),
            pltpu.VMEM(wanted.shape, jnp.int32),
            pltpu.VMEM(w_bilinear.shape, BF16),
            pltpu.VMEM(w_down.shape[::-1], BF16),
            pltpu.VMEM((2,) + w_up.shape, BF16),
            pltpu.VMEM(w_residual.shape, BF16),
            pltpu.VMEM(tile_coef.shape, BF16),
            pltpu.VMEM((2,) + tile, BF16),
            pltpu.VMEM((n_blocks, half_c, rows_b), BF16),
            pltpu.VMEM((blocks, half_c, rows_b), F32),
            pltpu.VMEM((4,) + tile, F32),
            pltpu.VMEM((2,) + tile, BF16),
            pltpu.VMEM((blocks, half_c, rows_b), BF16),
            pltpu.VMEM((entries + 1, half_c, rows_b), F32),
            pltpu.VMEM((n2,) + tile, F32),
            pltpu.VMEM((n2,) + tile, F32),
            pltpu.VMEM((n2,) + tile, BF16),
            pltpu.VMEM((n2,) + tile, BF16),
            pltpu.VMEM((2, rows, cols), BF16),
            pltpu.VMEM((2, rows, cols), BF16),
            pltpu.VMEM((edges, cols), BF16),
            pltpu.VMEM((n_edge, span, span), BF16),
            pltpu.VMEM((n_edge, span, cols), BF16),
            pltpu.SMEM(tile_source.shape[::-1], jnp.int32),
            pltpu.VMEM((entries, lanes), jnp.int32),
            pltpu.VMEM((1, lanes), jnp.int32),
            pltpu.SMEM((entries, lanes), jnp.int32),
            pltpu.SMEM((1, lanes), jnp.int32),
            pltpu.VMEM((rows // span, width, span), BF16),
            pltpu.VMEM((n_edge, width, span), BF16),
            pltpu.VMEM((edges, cols), BF16),
            dma((13 + n_edge,)),
            dma((4,)),
            dma((4,)),
            dma((n2,)),
            dma((n2,)),
            dma((n2,)),
            dma((n2,)),
            dma((4,)),
            dma((4,)),
            dma((4,)),
            dma((4,)),
            dma(()),
            dma(()),
            dma((n2,)),
            dma((n2,)),
            dma((4,)),
            dma((4,)),
            dma((rows // span, 4)),
            dma((n_edge,)),
            dma((n_edge,)),
            dma((n_edge,)),
            dma(()),
            dma((rows // span, 4)),
            dma((n_edge,)),
        ],
        compiler_params=pltpu.CompilerParams(
            collective_id=0, has_side_effects=True, vmem_limit_bytes=60 * 1024 * 1024
        ),
        name="interaction",
    )(
        tile_source.T,
        wanted,
        w_bilinear,
        edge_embed,
        w_down.T,
        w_up,
        w_residual,
        tile_coef,
        cotangent,
    )


def silu_slope(value):
    sig = jax.nn.sigmoid(value)
    return sig * (1.0 + value * (1.0 - sig))


def feat_total(value):
    return lax.psum(value, "feat")


def rep_total(value):
    return lax.psum(value, "rep")


def trade(payload):
    return lax.all_to_all(payload, "edge", split_axis=0, concat_axis=0, tiled=True)


def contract(values, piece_weight):
    piece = lax.all_gather(values, "feat", axis=1, tiled=True)
    return jnp.dot(
        piece, piece_weight(jnp.int32(0), piece.shape[1]), preferred_element_type=jnp.float32
    )


def on_device(
    edge_embed, w_down, w_bilinear, w_up, w_residual, tile_coef, tile_source, target_rows, cotangent
):
    edges_dev, columns = edge_embed.shape
    blocks_dev, tiles_half, block_rows, _ = tile_coef.shape
    width_tri = w_down.shape[1]
    peers = lax.axis_size("edge")
    copies = lax.axis_size("rep")
    my_edge = lax.axis_index("edge")
    my_rep = lax.axis_index("rep")
    my_feat = lax.axis_index("feat")
    capacity = 2 * blocks_dev * tiles_half // peers
    entries = blocks_dev * tiles_half
    grid = tile_source.reshape(peers, blocks_dev, copies, tiles_half)
    lists = lax.dynamic_index_in_dim(grid, my_rep, axis=2, keepdims=False).reshape(peers, entries)
    owners = lists // blocks_dev
    local_ids = lists % blocks_dev
    hits = owners == my_edge
    slot_send = jnp.cumsum(hits.astype(jnp.int32), axis=1) - 1
    slot_range = jnp.arange(capacity, dtype=jnp.int32)
    picked = hits[:, :, None] & (slot_send[:, :, None] == slot_range[None, None, :])
    send_local = jnp.sum(jnp.where(picked, local_ids[:, :, None], 0), axis=1)
    send_valid = jnp.any(picked, axis=1)
    my_list = lax.dynamic_index_in_dim(lists, my_edge, 0, keepdims=False)
    my_owner = my_list // blocks_dev
    order = jnp.arange(entries, dtype=jnp.int32)
    same_before = (my_owner[:, None] == my_owner[None, :]) & (order[None, :] < order[:, None])
    my_slot = jnp.sum(same_before.astype(jnp.int32), axis=1)
    pre_down = feat_total(jnp.dot(edge_embed, w_down, preferred_element_type=jnp.float32))
    down_own = jax.nn.silu(pre_down).astype(jnp.bfloat16)
    down_blocks = down_own.reshape(blocks_dev, block_rows, width_tri)
    arrived = trade(down_blocks[send_local])
    sources = arrived[my_owner, my_slot]
    sources = sources.reshape(blocks_dev, tiles_half, block_rows, width_tri)
    partial_tri = jnp.einsum(
        "bkij,bkjc->bic", tile_coef, sources, preferred_element_type=jnp.float32
    )
    partial_tri = partial_tri.reshape(edges_dev, width_tri)
    tri_sum = rep_total(partial_tri).astype(jnp.bfloat16)
    pre_bil = jnp.dot(tri_sum, w_bilinear, preferred_element_type=jnp.float32)
    mid_act = jax.nn.silu(pre_bil).astype(jnp.bfloat16)
    hidden = (
        edge_embed.astype(jnp.float32) + jnp.dot(mid_act, w_up, preferred_element_type=jnp.float32)
    ).astype(jnp.bfloat16)
    saved = []
    for layer in range(w_residual.shape[0]):
        weight = w_residual[layer]

        def rows_piece(start, count, weight=weight):
            return lax.dynamic_slice(weight, (start, my_feat * columns), (count, columns))

        pre_res = contract(hidden, rows_piece)
        hidden = (hidden.astype(jnp.float32) + jax.nn.silu(pre_res)).astype(jnp.bfloat16)
        saved.append(pre_res)
    grad_hidden = cotangent.astype(jnp.float32)
    for layer in range(w_residual.shape[0] - 1, -1, -1):
        dz_layer = (grad_hidden * silu_slope(saved[layer])).astype(jnp.bfloat16)
        weight = w_residual[layer]

        def cols_piece(start, count, weight=weight):
            return lax.dynamic_slice(weight, (my_feat * columns, start), (columns, count)).T

        grad_hidden = grad_hidden + contract(dz_layer, cols_piece)
    grad_hb = grad_hidden.astype(jnp.bfloat16)
    grad_mid = feat_total(jnp.dot(grad_hb, w_up.T, preferred_element_type=jnp.float32))
    grad_bil = (grad_mid * silu_slope(pre_bil)).astype(jnp.bfloat16)
    grad_tri_own = jnp.dot(grad_bil, w_bilinear.T, preferred_element_type=jnp.float32).astype(
        jnp.bfloat16
    )
    grad_blocks = grad_tri_own.reshape(blocks_dev, block_rows, width_tri)
    contrib = jnp.einsum(
        "bkij,bic->bkjc", tile_coef, grad_blocks, preferred_element_type=jnp.float32
    ).astype(jnp.bfloat16)
    contrib = contrib.reshape(entries, block_rows, width_tri)
    outgoing = (
        jnp.zeros((peers, capacity, block_rows, width_tri), jnp.bfloat16)
        .at[my_owner, my_slot]
        .set(contrib)
    )
    incoming = trade(outgoing).reshape(peers * capacity, block_rows, width_tri)
    block_range = jnp.arange(blocks_dev, dtype=jnp.int32)
    select = (
        (send_local[:, :, None] == block_range[None, None, :]) & send_valid[:, :, None]
    ).astype(jnp.bfloat16)
    select = select.reshape(peers * capacity, blocks_dev)
    grad_down = jnp.einsum("sl,sjc->ljc", select, incoming, preferred_element_type=jnp.float32)
    grad_down = grad_down.reshape(edges_dev, width_tri)
    grad_down = rep_total(grad_down)
    grad_pre = (grad_down * silu_slope(pre_down)).astype(jnp.bfloat16)
    grad_edge = (
        grad_hb.astype(jnp.float32)
        + jnp.dot(grad_pre, w_down.T, preferred_element_type=jnp.float32)
    ).astype(jnp.bfloat16)
    span_rows = edges_dev // peers
    turned = lax.all_to_all(grad_edge, "edge", split_axis=0, concat_axis=0, tiled=True)
    position = target_rows // edges_dev * span_rows + target_rows % span_rows
    grad_target = turned[position]
    return (hidden, grad_target)


def solution(mesh):
    placed = (
        P(("grp", "edge"), "feat"),
        P("feat", None),
        P(),
        P(None, "feat"),
        P(),
        P(("grp", "edge"), "rep", None, None),
        P("grp", None),
        P(("grp", "edge")),
        P(("grp", "edge"), "feat"),
    )
    fits = mesh.shape["feat"] == 2 and mesh.shape["rep"] == 2 and mesh.shape["edge"] in (4, 8)
    return jax.shard_map(
        fused if fits else on_device,
        mesh=mesh,
        in_specs=placed,
        out_specs=(P(("grp", "edge"), "feat"), P(("grp", "edge"), "feat")),
        check_vma=False,
    )
```

```python
import functools

import jax
import jax.numpy as jnp
from jax import lax
from jax.experimental import pallas as pl
from jax.experimental.pallas import tpu as pltpu
from jax.sharding import PartitionSpec as P

MESH = pl.DeviceIdType.MESH
F32 = jnp.float32
BF16 = jnp.bfloat16


def mm(a, b, ca, cb):
    return lax.dot_general(a, b, (((ca,), (cb,)), ((), ())), preferred_element_type=F32)


def slope(value):
    sig = jax.nn.sigmoid(value)
    return sig * (1.0 + value * (1.0 - sig))


def block_kernel(
    n_edge,
    source_hbm,
    wanted_hbm,
    bil_hbm,
    edge_hbm,
    down_hbm,
    up_hbm,
    res_hbm,
    coef_hbm,
    cot_hbm,
    edge_out,
    grad_out,
    emb,
    emb_x,
    pd_part,
    pd_in,
    cot,
    wanted,
    w_bil,
    w_down,
    w_up,
    w_res,
    coef,
    down_mine,
    table,
    tri_part,
    tri_out,
    tri_in,
    bil_mine,
    grad_tri,
    chain,
    pair_out,
    pair_in,
    red_out,
    red_in,
    out_mine,
    ge,
    turned,
    picks,
    hb_perm,
    source,
    seen,
    newest,
    before,
    last,
    gp_mine,
    gp_in,
    local_sem,
    x_send,
    x_recv,
    tab_send,
    tab_recv,
    core_send,
    core_recv,
    tri_send,
    tri_recv,
    bil_send,
    bil_recv,
    pair_send,
    pair_recv,
    red_send,
    red_recv,
    out_send,
    out_recv,
    ge_send,
    ge_recv,
    fin_send,
    fin_recv,
    fin_local,
    gp_send,
    gp_recv,
):
    g = lax.axis_index("grp")
    e = lax.axis_index("edge")
    f = lax.axis_index("feat")
    r = lax.axis_index("rep")
    of = 1 - f
    orr = 1 - r
    s = 2 * f + r
    blocks, tiles, rows_b, _ = coef.shape
    bpd = blocks // 4
    rows = emb.shape[1]
    half_c = table.shape[1]
    span = turned.shape[0] // n_edge
    spd = rows // span
    hs = span // 2

    def peer(d, df, dr):
        return (g, lax.rem(e + d, n_edge), of if df else f, orr if dr else r)

    def remote(src, dst, ss, rs, dev):
        return pltpu.make_async_remote_copy(
            src_ref=src, dst_ref=dst, send_sem=ss, recv_sem=rs, device_id=dev, device_id_type=MESH
        )

    def mine(who):
        return pl.ds(who * rows, rows)

    partner_rows = mine(2 * of + r)
    local = [
        pltpu.make_async_copy(down_hbm, w_down, local_sem.at[0]),
        pltpu.make_async_copy(edge_hbm.at[mine(s)], emb.at[f], local_sem.at[1]),
        pltpu.make_async_copy(up_hbm, w_up.at[f], local_sem.at[2]),
        pltpu.make_async_copy(coef_hbm, coef, local_sem.at[3]),
        pltpu.make_async_copy(res_hbm, w_res, local_sem.at[4]),
        pltpu.make_async_copy(cot_hbm.at[mine(s)], cot.at[f], local_sem.at[5]),
        pltpu.make_async_copy(bil_hbm, w_bil, local_sem.at[7]),
        pltpu.make_async_copy(wanted_hbm, wanted, local_sem.at[8]),
        pltpu.make_async_copy(edge_hbm.at[partner_rows], emb_x, local_sem.at[9]),
        pltpu.make_async_copy(source_hbm, source, local_sem.at[10]),
    ]
    for copy in local:
        copy.start()

    barrier = pltpu.get_barrier_semaphore()
    others = 0
    for d in range(n_edge):
        for df in range(2):
            for dr in range(2):
                if d or df or dr:
                    pl.semaphore_signal(
                        barrier, inc=1, device_id=peer(d, df, dr), device_id_type=MESH
                    )
                    others += 1
    local[0].wait()
    local[1].wait()
    local[8].wait()
    wd = w_down[...]
    pd_part[...] = mm(wd, emb_x[...], 1, 1)
    own_part = mm(wd, emb[f], 1, 1)
    pl.semaphore_wait(barrier, others)

    across = peer(0, 1, 0)
    xs = [
        remote(pd_part, pd_in, x_send.at[0], x_recv.at[0], across),
        remote(emb_x, emb.at[f], x_send.at[1], x_recv.at[1], across),
        remote(up_hbm, w_up.at[f], x_send.at[2], x_recv.at[2], across),
        remote(cot_hbm.at[partner_rows], cot.at[f], x_send.at[3], x_recv.at[3], across),
    ]
    xs[0].start()
    xs[0].wait_recv()
    pre_down = own_part + pd_in[...]
    down = jax.nn.silu(pre_down).astype(BF16)
    for h in range(2):
        for b in range(bpd):
            down_mine[h, b] = down[h * half_c : (h + 1) * half_c, b * rows_b : (b + 1) * rows_b]

    def region(ed, who):
        return pl.ds(ed * blocks + who * bpd, bpd)

    tabs = []
    for i in range(1, 2 * n_edge):
        d, df = i // 2, i % 2
        copy = remote(
            down_mine.at[of if df else f],
            table.at[region(e, s)],
            tab_send.at[i],
            tab_recv.at[i],
            peer(d, df, 0),
        )
        copy.start()
        tabs.append(copy)
    own = remote(
        down_mine.at[f], table.at[region(e, s)], core_send.at[0], core_recv.at[0], peer(0, 0, 1)
    )
    own.start()
    xs[1].start()
    xs[2].start()
    table[region(e, s)] = down_mine[f]
    local[9].wait()
    entries = blocks * tiles
    lanes = newest.shape[1]
    ids = lax.broadcasted_iota(jnp.int32, (1, lanes), 1)
    latest = jnp.zeros((1, lanes), jnp.int32)
    for t in range(entries):
        hit = ids == source[r * tiles + t % tiles, e * blocks + t // tiles]
        seen[t : t + 1, :] = jnp.where(hit, latest, 0)
        latest = jnp.where(hit, t + 1, latest)
    newest[...] = latest
    seen[...] = jnp.broadcast_to(jnp.max(seen[...], axis=1, keepdims=True), seen.shape)
    lists = [
        pltpu.make_async_copy(seen, before, local_sem.at[11]),
        pltpu.make_async_copy(newest, last, local_sem.at[12]),
    ]
    for copy in lists:
        copy.start()
    cores = [own]
    for i in range(1, 2 * n_edge):
        d, df = i // 2, i % 2
        tabs[i - 1].wait_recv()
        place = region(lax.rem(e + n_edge - d, n_edge), 2 * (of if df else f) + r)
        copy = remote(
            table.at[place], table.at[place], core_send.at[i], core_recv.at[i], peer(0, 0, 1)
        )
        copy.start()
        cores.append(copy)
    local[3].wait()
    for copy in cores:
        copy.wait_recv()

    xs[3].start()

    def forward(n, _):
        total = jnp.zeros((half_c, rows_b), F32)
        for k in range(tiles):
            total += mm(table[source[r * tiles + k, e * blocks + n]], coef[n, k], 1, 1)
        tri_part[n] = total
        tri_out[n] = total.astype(BF16)
        return 0

    lax.fori_loop(0, blocks, forward, 0)
    tris = []
    for i in range(1, 4):
        df, dr = i // 2, i % 2
        to = 2 * (of if df else f) + (orr if dr else r)
        copy = remote(
            tri_out.at[pl.ds(to * bpd, bpd)],
            tri_in.at[i],
            tri_send.at[i],
            tri_recv.at[i],
            peer(0, df, dr),
        )
        copy.start()
        tris.append(copy)
    for copy in tris:
        copy.wait_recv()
    near = tri_part[pl.ds(s * bpd, bpd)] + tri_in[1].astype(F32)
    far = tri_in[2].astype(F32) + tri_in[3].astype(F32)
    low = jnp.where(f == 0, near, far)
    high = jnp.where(f == 0, far, near)
    tri = jnp.concatenate(
        [jnp.concatenate([low[b], high[b]], axis=0) for b in range(bpd)], axis=1
    ).astype(BF16)
    local[6].wait()
    wb = w_bil[...]
    pre_bil = mm(wb, tri, 0, 0)
    mid = jax.nn.silu(pre_bil).astype(BF16)
    local[2].wait()
    xs[2].wait_recv()
    xs[1].wait_recv()
    embed = jnp.concatenate([emb[0], emb[1]], axis=1)
    wu = jnp.concatenate([w_up[0], w_up[1]], axis=1)
    hidden = (embed.astype(F32) + mm(mid, wu, 0, 0)).astype(BF16)
    local[4].wait()
    saved = []
    for layer in range(w_res.shape[0]):
        pre = mm(hidden, w_res[layer], 1, 0)
        hidden = (hidden.astype(F32) + jax.nn.silu(pre)).astype(BF16)
        saved.append(slope(pre))
    cols = emb.shape[2]
    for h in range(2):
        out_mine[h] = hidden[:, h * cols : (h + 1) * cols]
    outs = []
    for i in range(1, 3):
        copy = remote(
            out_mine.at[of if i == 2 else f],
            edge_out.at[mine(s)],
            out_send.at[i],
            out_recv.at[i],
            peer(0, i // 2, i % 2),
        )
        copy.start()
        outs.append(copy)
    out_local = pltpu.make_async_copy(out_mine.at[f], edge_out.at[mine(s)], local_sem.at[6])
    out_local.start()
    local[5].wait()
    xs[3].wait_recv()
    grad = jnp.concatenate([cot[0], cot[1]], axis=1).astype(F32)
    for layer in range(w_res.shape[0] - 1, -1, -1):
        dz = (grad * saved[layer]).astype(BF16)
        grad = grad + mm(dz, w_res[layer], 1, 1)
    grad_hb = grad.astype(BF16)
    grad_bil = (mm(wu, grad_hb, 1, 1) * slope(pre_bil)).astype(BF16)
    grad_t = mm(wb, grad_bil, 1, 0).astype(BF16)
    for h in range(2):
        for b in range(bpd):
            bil_mine[h, b] = grad_t[h * half_c : (h + 1) * half_c, b * rows_b : (b + 1) * rows_b]
    bils = []
    for i in range(1, 4):
        df, dr = i // 2, i % 2
        copy = remote(
            bil_mine.at[of if df else f],
            grad_tri.at[pl.ds(s * bpd, bpd)],
            bil_send.at[i],
            bil_recv.at[i],
            peer(0, df, dr),
        )
        copy.start()
        bils.append(copy)
    for h in range(2):
        ge[h] = grad_hb[:, h * cols : (h + 1) * cols]
    sends = []
    for j in range(spd):
        q = s * spd + j
        d = lax.rem(q - e + n_edge, n_edge)
        for df in range(2):
            for dr in range(2):
                rt = orr if dr else r
                fr = of if df else f
                src = ge.at[fr, pl.ds(j * span + rt * hs, hs)]
                dst = turned.at[pl.ds(e * span + rt * hs, hs)]
                copy = remote(
                    src,
                    dst,
                    ge_send.at[j, 2 * df + dr],
                    ge_recv.at[d],
                    (g, q, fr, rt),
                )
                if df or dr:
                    copy.start()
                    sends.append((copy, None))
                else:
                    keep = pltpu.make_async_copy(src, dst, fin_local)

                    @pl.when(q == e)
                    def _(keep=keep):
                        keep.start()
                        keep.wait()

                    @pl.when(q != e)
                    def _(copy=copy):
                        copy.start()

                    sends.append((copy, q != e))
    grad_tri[pl.ds(s * bpd, bpd)] = bil_mine[f]
    chain[0] = jnp.zeros((half_c, rows_b), F32)
    for copy in lists:
        copy.wait()
    for copy in bils:
        copy.wait_recv()

    def backward(n, _):
        block = grad_tri[n]
        parts = [mm(block, coef[n, k], 1, 0) for k in range(tiles)]
        for k in range(tiles):
            t = n * tiles + k
            chain[t + 1] = parts[k] + chain[before[t, 0]]
        return 0

    lax.fori_loop(0, blocks, backward, 0)
    for i in range(2 * n_edge):
        for b in range(bpd):
            block_id = (i // 2) * blocks + (2 * (i % 2) + orr) * bpd + b
            pair_out[i, b] = chain[last[0, block_id]].astype(BF16)
    pair = remote(pair_out, pair_in, pair_send, pair_recv, peer(0, 0, 1))
    pair.start()
    pair.wait_recv()
    for i in range(2 * n_edge):
        for b in range(bpd):
            block_id = (i // 2) * blocks + (2 * (i % 2) + r) * bpd + b
            red_out[i, b] = (chain[last[0, block_id]] + pair_in[i, b].astype(F32)).astype(BF16)
    reds = []
    for i in range(1, 2 * n_edge):
        d, df = i // 2, i % 2
        slot = 2 * lax.rem(e + d, n_edge) + (of if df else f)
        copy = remote(
            red_out.at[slot], red_in.at[i], red_send.at[i], red_recv.at[i], peer(d, df, 0)
        )
        copy.start()
        reds.append(copy)
    for copy in reds:
        copy.wait_recv()
    near = red_out[2 * e + f].astype(F32)
    far = red_in[1].astype(F32)
    for d in range(1, n_edge):
        near += red_in[2 * d].astype(F32)
        far += red_in[2 * d + 1].astype(F32)
    low = jnp.where(f == 0, near, far)
    high = jnp.where(f == 0, far, near)
    grad_down = jnp.concatenate(
        [jnp.concatenate([low[b], high[b]], axis=0) for b in range(bpd)], axis=1
    )
    grad_pre = (grad_down * slope(pre_down)).astype(BF16)
    given = []
    for j in range(spd):
        gp_mine[j] = grad_pre[:, j * span : (j + 1) * span]
        q = s * spd + j
        d = lax.rem(q - e + n_edge, n_edge)
        for df in range(2):
            for dr in range(2):
                copy = remote(
                    gp_mine.at[j],
                    gp_in.at[e],
                    gp_send.at[j, 2 * df + dr],
                    gp_recv.at[d],
                    (g, q, of if df else f, orr if dr else r),
                )
                if df or dr:
                    copy.start()
                    given.append((copy, None))
                else:

                    @pl.when(q == e)
                    def _(j=j):
                        gp_in[e] = gp_mine[j]

                    @pl.when(q != e)
                    def _(copy=copy):
                        copy.start()

                    given.append((copy, q != e))
    fins = []
    for d in range(n_edge):
        p = lax.rem(e + n_edge - d, n_edge)
        place = pl.ds(p * span + r * hs, hs)
        arrive = remote(
            turned.at[place], turned.at[place], ge_send.at[0, 0], ge_recv.at[d], peer(0, 0, 1)
        )
        if d:
            arrive.wait_recv()
        else:

            @pl.when(s != e // spd)
            def _(arrive=arrive):
                arrive.wait_recv()

        copy = remote(
            turned.at[place], turned.at[place], fin_send.at[d], fin_recv.at[d], peer(0, 0, 1)
        )
        copy.start()
        fins.append(copy)
    relay_rows = mine(2 * of + r)
    outs[1].wait_recv()
    relay = remote(
        edge_out.at[relay_rows], edge_out.at[relay_rows], out_send.at[3], out_recv.at[3], peer(0, 0, 1)
    )
    relay.start()
    local[7].wait()
    for d in range(n_edge):
        p = lax.rem(e + n_edge - d, n_edge)
        fins[d].wait_recv()
        wish = wanted[p] - (p * turned.shape[0] + e * span)
        slot = lax.broadcasted_iota(jnp.int32, (span, span), 0)
        pick = jnp.where(slot == wish, 1.0, 0.0).astype(BF16)
        picks[d] = pick
        hb_perm[d] = mm(pick, turned[pl.ds(p * span, span)], 0, 0).astype(BF16)
    for d in range(n_edge):
        p = lax.rem(e + n_edge - d, n_edge)
        arrive = remote(gp_mine.at[0], gp_in.at[p], gp_send.at[0, 0], gp_recv.at[d], peer(0, 0, 1))
        if d:
            arrive.wait_recv()
        else:

            @pl.when(s != e // spd)
            def _(arrive=arrive):
                arrive.wait_recv()

        moved = mm(gp_in[p], picks[d], 1, 0).astype(BF16)
        place = pl.ds(p * span, span)
        grad_out[place] = (hb_perm[d].astype(F32) + mm(moved, wd, 0, 0)).astype(BF16)
    relay.wait_recv()
    outs[0].wait_recv()
    out_local.wait()
    for copy in xs + tabs + cores + tris + outs + [relay] + bils + [pair] + reds + fins:
        copy.wait_send()
    for copy, when in sends + given:
        if when is None:
            copy.wait_send()
        else:

            @pl.when(when)
            def _(copy=copy):
                copy.wait_send()


def fused(
    edge_embed, w_down, w_bilinear, w_up, w_residual, tile_coef, tile_source, target_rows, cotangent
):
    n_edge = lax.axis_size("edge")
    edges, cols = edge_embed.shape
    blocks, tiles, rows_b, _ = tile_coef.shape
    width = w_down.shape[1]
    half_c = width // 2
    bpd = blocks // 4
    rows = edges // 4
    span = edges // n_edge
    n_blocks = n_edge * blocks
    entries = blocks * tiles
    lanes = -(-n_blocks // 128) * 128
    wanted = target_rows.reshape(n_edge, 1, span)
    fixed = pl.BlockSpec(memory_space=pltpu.HBM)
    hbm = pl.BlockSpec(memory_space=pl.ANY)
    dma = pltpu.SemaphoreType.DMA
    tile = (bpd, half_c, rows_b)
    n2 = 2 * n_edge
    return pl.pallas_call(
        functools.partial(block_kernel, n_edge),
        out_shape=[pltpu.VMEM((edges, cols), BF16)] * 2,
        in_specs=[fixed] * 9,
        out_specs=[hbm, pl.BlockSpec(memory_space=pltpu.VMEM)],
        scratch_shapes=[
            pltpu.VMEM((2, rows, cols), BF16),
            pltpu.VMEM((rows, cols), BF16),
            pltpu.VMEM((width, rows), F32),
            pltpu.VMEM((width, rows), F32),
            pltpu.VMEM((2, rows, cols), BF16),
            pltpu.VMEM(wanted.shape, jnp.int32),
            pltpu.VMEM(w_bilinear.shape, BF16),
            pltpu.VMEM(w_down.shape[::-1], BF16),
            pltpu.VMEM((2,) + w_up.shape, BF16),
            pltpu.VMEM(w_residual.shape, BF16),
            pltpu.VMEM(tile_coef.shape, BF16),
            pltpu.VMEM((2,) + tile, BF16),
            pltpu.VMEM((n_blocks, half_c, rows_b), BF16),
            pltpu.VMEM((blocks, half_c, rows_b), F32),
            pltpu.VMEM((blocks, half_c, rows_b), BF16),
            pltpu.VMEM((4,) + tile, BF16),
            pltpu.VMEM((2,) + tile, BF16),
            pltpu.VMEM((blocks, half_c, rows_b), BF16),
            pltpu.VMEM((entries + 1, half_c, rows_b), F32),
            pltpu.VMEM((n2,) + tile, BF16),
            pltpu.VMEM((n2,) + tile, BF16),
            pltpu.VMEM((n2,) + tile, BF16),
            pltpu.VMEM((n2,) + tile, BF16),
            pltpu.VMEM((2, rows, cols), BF16),
            pltpu.VMEM((2, rows, cols), BF16),
            pltpu.VMEM((edges, cols), BF16),
            pltpu.VMEM((n_edge, span, span), BF16),
            pltpu.VMEM((n_edge, span, cols), BF16),
            pltpu.SMEM(tile_source.shape[::-1], jnp.int32),
            pltpu.VMEM((entries, lanes), jnp.int32),
            pltpu.VMEM((1, lanes), jnp.int32),
            pltpu.SMEM((entries, lanes), jnp.int32),
            pltpu.SMEM((1, lanes), jnp.int32),
            pltpu.VMEM((rows // span, width, span), BF16),
            pltpu.VMEM((n_edge, width, span), BF16),
            dma((13,)),
            dma((4,)),
            dma((4,)),
            dma((n2,)),
            dma((n2,)),
            dma((n2,)),
            dma((n2,)),
            dma((4,)),
            dma((4,)),
            dma((4,)),
            dma((4,)),
            dma(()),
            dma(()),
            dma((n2,)),
            dma((n2,)),
            dma((4,)),
            dma((4,)),
            dma((rows // span, 4)),
            dma((n_edge,)),
            dma((n_edge,)),
            dma((n_edge,)),
            dma(()),
            dma((rows // span, 4)),
            dma((n_edge,)),
        ],
        compiler_params=pltpu.CompilerParams(
            collective_id=0, has_side_effects=True, vmem_limit_bytes=60 * 1024 * 1024
        ),
        name="interaction",
    )(
        tile_source.T,
        wanted,
        w_bilinear,
        edge_embed,
        w_down.T,
        w_up,
        w_residual,
        tile_coef,
        cotangent,
    )


def silu_slope(value):
    sig = jax.nn.sigmoid(value)
    return sig * (1.0 + value * (1.0 - sig))


def feat_total(value):
    return lax.psum(value, "feat")


def rep_total(value):
    return lax.psum(value, "rep")


def trade(payload):
    return lax.all_to_all(payload, "edge", split_axis=0, concat_axis=0, tiled=True)


def contract(values, piece_weight):
    piece = lax.all_gather(values, "feat", axis=1, tiled=True)
    return jnp.dot(
        piece, piece_weight(jnp.int32(0), piece.shape[1]), preferred_element_type=jnp.float32
    )


def on_device(
    edge_embed, w_down, w_bilinear, w_up, w_residual, tile_coef, tile_source, target_rows, cotangent
):
    edges_dev, columns = edge_embed.shape
    blocks_dev, tiles_half, block_rows, _ = tile_coef.shape
    width_tri = w_down.shape[1]
    peers = lax.axis_size("edge")
    copies = lax.axis_size("rep")
    my_edge = lax.axis_index("edge")
    my_rep = lax.axis_index("rep")
    my_feat = lax.axis_index("feat")
    capacity = 2 * blocks_dev * tiles_half // peers
    entries = blocks_dev * tiles_half
    grid = tile_source.reshape(peers, blocks_dev, copies, tiles_half)
    lists = lax.dynamic_index_in_dim(grid, my_rep, axis=2, keepdims=False).reshape(peers, entries)
    owners = lists // blocks_dev
    local_ids = lists % blocks_dev
    hits = owners == my_edge
    slot_send = jnp.cumsum(hits.astype(jnp.int32), axis=1) - 1
    slot_range = jnp.arange(capacity, dtype=jnp.int32)
    picked = hits[:, :, None] & (slot_send[:, :, None] == slot_range[None, None, :])
    send_local = jnp.sum(jnp.where(picked, local_ids[:, :, None], 0), axis=1)
    send_valid = jnp.any(picked, axis=1)
    my_list = lax.dynamic_index_in_dim(lists, my_edge, 0, keepdims=False)
    my_owner = my_list // blocks_dev
    order = jnp.arange(entries, dtype=jnp.int32)
    same_before = (my_owner[:, None] == my_owner[None, :]) & (order[None, :] < order[:, None])
    my_slot = jnp.sum(same_before.astype(jnp.int32), axis=1)
    pre_down = feat_total(jnp.dot(edge_embed, w_down, preferred_element_type=jnp.float32))
    down_own = jax.nn.silu(pre_down).astype(jnp.bfloat16)
    down_blocks = down_own.reshape(blocks_dev, block_rows, width_tri)
    arrived = trade(down_blocks[send_local])
    sources = arrived[my_owner, my_slot]
    sources = sources.reshape(blocks_dev, tiles_half, block_rows, width_tri)
    partial_tri = jnp.einsum(
        "bkij,bkjc->bic", tile_coef, sources, preferred_element_type=jnp.float32
    )
    partial_tri = partial_tri.reshape(edges_dev, width_tri)
    tri_sum = rep_total(partial_tri).astype(jnp.bfloat16)
    pre_bil = jnp.dot(tri_sum, w_bilinear, preferred_element_type=jnp.float32)
    mid_act = jax.nn.silu(pre_bil).astype(jnp.bfloat16)
    hidden = (
        edge_embed.astype(jnp.float32) + jnp.dot(mid_act, w_up, preferred_element_type=jnp.float32)
    ).astype(jnp.bfloat16)
    saved = []
    for layer in range(w_residual.shape[0]):
        weight = w_residual[layer]

        def rows_piece(start, count, weight=weight):
            return lax.dynamic_slice(weight, (start, my_feat * columns), (count, columns))

        pre_res = contract(hidden, rows_piece)
        hidden = (hidden.astype(jnp.float32) + jax.nn.silu(pre_res)).astype(jnp.bfloat16)
        saved.append(pre_res)
    grad_hidden = cotangent.astype(jnp.float32)
    for layer in range(w_residual.shape[0] - 1, -1, -1):
        dz_layer = (grad_hidden * silu_slope(saved[layer])).astype(jnp.bfloat16)
        weight = w_residual[layer]

        def cols_piece(start, count, weight=weight):
            return lax.dynamic_slice(weight, (my_feat * columns, start), (columns, count)).T

        grad_hidden = grad_hidden + contract(dz_layer, cols_piece)
    grad_hb = grad_hidden.astype(jnp.bfloat16)
    grad_mid = feat_total(jnp.dot(grad_hb, w_up.T, preferred_element_type=jnp.float32))
    grad_bil = (grad_mid * silu_slope(pre_bil)).astype(jnp.bfloat16)
    grad_tri_own = jnp.dot(grad_bil, w_bilinear.T, preferred_element_type=jnp.float32).astype(
        jnp.bfloat16
    )
    grad_blocks = grad_tri_own.reshape(blocks_dev, block_rows, width_tri)
    contrib = jnp.einsum(
        "bkij,bic->bkjc", tile_coef, grad_blocks, preferred_element_type=jnp.float32
    ).astype(jnp.bfloat16)
    contrib = contrib.reshape(entries, block_rows, width_tri)
    outgoing = (
        jnp.zeros((peers, capacity, block_rows, width_tri), jnp.bfloat16)
        .at[my_owner, my_slot]
        .set(contrib)
    )
    incoming = trade(outgoing).reshape(peers * capacity, block_rows, width_tri)
    block_range = jnp.arange(blocks_dev, dtype=jnp.int32)
    select = (
        (send_local[:, :, None] == block_range[None, None, :]) & send_valid[:, :, None]
    ).astype(jnp.bfloat16)
    select = select.reshape(peers * capacity, blocks_dev)
    grad_down = jnp.einsum("sl,sjc->ljc", select, incoming, preferred_element_type=jnp.float32)
    grad_down = grad_down.reshape(edges_dev, width_tri)
    grad_down = rep_total(grad_down)
    grad_pre = (grad_down * silu_slope(pre_down)).astype(jnp.bfloat16)
    grad_edge = (
        grad_hb.astype(jnp.float32)
        + jnp.dot(grad_pre, w_down.T, preferred_element_type=jnp.float32)
    ).astype(jnp.bfloat16)
    span_rows = edges_dev // peers
    turned = lax.all_to_all(grad_edge, "edge", split_axis=0, concat_axis=0, tiled=True)
    position = target_rows // edges_dev * span_rows + target_rows % span_rows
    grad_target = turned[position]
    return (hidden, grad_target)


def solution(mesh):
    placed = (
        P(("grp", "edge"), "feat"),
        P("feat", None),
        P(),
        P(None, "feat"),
        P(),
        P(("grp", "edge"), "rep", None, None),
        P("grp", None),
        P(("grp", "edge")),
        P(("grp", "edge"), "feat"),
    )
    fits = mesh.shape["feat"] == 2 and mesh.shape["rep"] == 2 and mesh.shape["edge"] in (4, 8)
    return jax.shard_map(
        fused if fits else on_device,
        mesh=mesh,
        in_specs=placed,
        out_specs=(P(("grp", "edge"), "feat"), P(("grp", "edge"), "feat")),
        check_vma=False,
    )
```
